256 devices in a mesh: mem: 2 (over z_hi), tx: 16 (over z_lo, y), ty: 8 (over x, core).
Axes of the slice: x: 4, y: 4, z: 8 (z_hi: 2, z_lo: 4; z = z_hi * 4 + z_lo), core: 2. Of those that a mesh axis runs over, the one named last changes fastest.
Arguments:
- static_control: bfloat16 [768, 384, 128], P('tx', 'ty', 'mem'), may hold values from -6 to 6
- member_control: bfloat16 [4, 768, 384, 128], P('mem', 'tx', 'ty'), may hold values from -6 to 6
- perturbations: bfloat16 [4, 768, 384, 128], P('mem', 'tx', 'ty'), may hold values from -2.5 to 2.5
- departures: bfloat16 [768, 384, 128], P('tx', 'ty'), may hold values from -6 to 6
- obs_weight: bfloat16 [768, 384, 128], P('tx', 'ty'), may hold values from 0.25 to 2
- static_kx: bfloat16 [49], replicated, may hold values from 0.08984375 to 0.25976562
- static_ky: bfloat16 [49], replicated, may hold values from 0.08984375 to 0.25976562
- local_kx: bfloat16 [97], replicated, may hold values from 0.059814453 to 0.1796875
- local_ky: bfloat16 [97], replicated, may hold values from 0.059814453 to 0.1796875
- static_vertical: bfloat16 [128, 128], replicated, may hold values from -0.5 to 0.5
- local_vertical: bfloat16 [128, 128], replicated, may hold values from -0.5 to 0.5
Outputs:
- grad_static: bfloat16 [768, 384, 128], P('tx', 'ty', 'mem')
- grad_members: bfloat16 [4, 768, 384, 128], P('mem', 'tx', 'ty')
The draws below stay inside these ranges and needn't reach their ends.
All inputs are finite; a program needn't handle non-finite values.
Results may differ from the reference program's by a relative error of at most 0.0055.
Values may be sent and summed in bfloat16 or wider, within the bound.
No kernel may reach another device: no remote copies, remote signals or barrier semaphores. Data moves between devices by JAX's collectives and lax.ppermute only.
A program may use at most 64 MiB of HBM per device.

```python
import math
import jax
import jax.numpy as jnp
from jax import lax

TILE = 48
LEV = 128
MEMBERS = 4
NX = 768
NY = 384
RS = 24
RL = 48


def block_levels(key, shape, shards, low, largest):
    def one(position, blocks):
        draws = jax.random.uniform(jax.random.fold_in(jax.random.fold_in(key, 6), position), (blocks,), jnp.float32, low / len(shards), largest / len(shards))
        return jnp.repeat(jnp.exp(draws), shape[position] // blocks).reshape((-1,) + (1,) * (len(shape) - position - 1))

    loudness = one(*shards[0])
    for cut in shards[1:]:
        loudness = loudness * one(*cut)
    return loudness


def centred(key, shape, deviation, bound, split=(), held_as=jnp.bfloat16):
    values = deviation * jax.random.normal(key, shape, jnp.float32)
    if split:
        values = values * block_levels(key, shape, split, -0.22, 0.18)
    return jnp.clip(values, -bound, bound).astype(held_as)


def setup_inputs(seed: int = 0) -> dict:
    arg_keys = jax.random.split(jax.random.key(seed), 12)
    return {
        "static_control": centred(arg_keys[0], (NX, NY, LEV), 1.0, 6.0, ((0, 16), (1, 8), (2, 2))),
        "member_control": centred(arg_keys[1], (MEMBERS, NX, NY, LEV), 1.0, 6.0, ((0, 2), (1, 16), (2, 8))),
        "perturbations": centred(arg_keys[2], (MEMBERS, NX, NY, LEV), 0.35, 2.5, ((0, 2), (1, 16), (2, 8))),
        "departures": centred(arg_keys[3], (NX, NY, LEV), 1.0, 6.0, ((0, 16), (1, 8))),
        "obs_weight": jnp.clip(jnp.exp(math.log(2.0) - 2.0794415 * jax.random.uniform(arg_keys[4], (NX, NY, LEV), jnp.float32) ** block_levels(arg_keys[4], (NX, NY, LEV), ((0, 16), (1, 8)), -0.2, 0.2)), 0.25, 2.0).astype(jnp.bfloat16),
        "static_kx": jnp.clip(jax.random.uniform(arg_keys[5], (2 * RS + 1,), jnp.float32, 0.08984375, 0.25976562), 0.08984375, 0.25976562).astype(jnp.bfloat16),
        "static_ky": jnp.clip(jax.random.uniform(arg_keys[6], (2 * RS + 1,), jnp.float32, 0.08984375, 0.25976562), 0.08984375, 0.25976562).astype(jnp.bfloat16),
        "local_kx": jnp.clip(jax.random.uniform(arg_keys[7], (2 * RL + 1,), jnp.float32, 0.059814453, 0.1796875), 0.059814453, 0.1796875).astype(jnp.bfloat16),
        "local_ky": jnp.clip(jax.random.uniform(arg_keys[8], (2 * RL + 1,), jnp.float32, 0.059814453, 0.1796875), 0.059814453, 0.1796875).astype(jnp.bfloat16),
        "static_vertical": centred(arg_keys[9], (LEV, LEV), LEV ** -0.5, 0.5),
        "local_vertical": centred(arg_keys[10], (LEV, LEV), LEV ** -0.5, 0.5),
    }


def einsum_spec(rank_count, axis_pos):
    letters = "abcdefg"[:rank_count]
    result_letters = letters[:axis_pos] + "z" + letters[axis_pos + 1:]
    return letters + "," + letters[axis_pos] + "z->" + result_letters


def toeplitz(kernel, rows_in, cols_out, offset_lag):
    row_index = jnp.arange(rows_in, dtype=jnp.int32)[:, None, None]
    col_index = jnp.arange(cols_out, dtype=jnp.int32)[None, :, None]
    tap_count = kernel.shape[0]
    tap_index = jnp.arange(tap_count, dtype=jnp.int32)[None, None, :]
    hits = (row_index - col_index + offset_lag) == tap_index
    spread = jnp.where(hits, kernel.astype(jnp.float32)[None, None, :], jnp.zeros((), jnp.float32))
    return jnp.sum(spread, axis=2).astype(kernel.dtype)


def filter_line(field, kernel, axis_pos):
    sizes_in = field.shape
    block_count = sizes_in[axis_pos] // TILE
    blocked = field.reshape(sizes_in[:axis_pos] + (block_count, TILE) + sizes_in[axis_pos + 1:])
    widths = [(0, 0)] * blocked.ndim
    widths[axis_pos] = (1, 1)
    padded = jnp.pad(blocked, widths).astype(jnp.float32)
    radius = (kernel.shape[0] - 1) // 2
    einsum_form = einsum_spec(blocked.ndim, axis_pos + 1)
    summed = jnp.zeros(blocked.shape, jnp.float32)
    for offset in (-1, 0, 1):
        window = lax.slice_in_dim(padded, 1 + offset, 1 + offset + block_count, axis=axis_pos)
        matrix = toeplitz(kernel, TILE, TILE, radius + offset * TILE).astype(jnp.float32)
        summed = summed + jnp.einsum(einsum_form, window, matrix)
    return summed.reshape(sizes_in)


def horizontal(field, kernel_x, kernel_y):
    first_pass = filter_line(field, kernel_x, 0).astype(jnp.bfloat16)
    return filter_line(first_pass, kernel_y, 1).astype(jnp.bfloat16)


def reference(static_control, member_control, perturbations, departures, obs_weight, static_kx, static_ky, local_kx, local_ky, static_vertical, local_vertical):
    flat_shape = (NX * NY, LEV)
    static_filtered = horizontal(static_control, static_kx, static_ky)
    increment = jnp.dot(static_filtered.reshape(flat_shape), static_vertical.T, preferred_element_type=jnp.float32)

    def forward(carry, member_pair):
        control, member = member_pair
        member_filtered = horizontal(control, local_kx, local_ky)
        localized = jnp.dot(member_filtered.reshape(flat_shape), local_vertical.T, preferred_element_type=jnp.float32)
        return carry + member.reshape(flat_shape).astype(jnp.float32) * localized, None

    increment, unused = lax.scan(forward, increment, (member_control, perturbations))
    residual = (obs_weight.reshape(flat_shape).astype(jnp.float32) * (increment - departures.reshape(flat_shape).astype(jnp.float32))).astype(jnp.bfloat16)
    static_back = jnp.dot(residual, static_vertical, preferred_element_type=jnp.float32).astype(jnp.bfloat16).reshape(NX, NY, LEV)
    static_pulled = horizontal(static_back, static_kx[::-1], static_ky[::-1])
    grad_static = (static_control.astype(jnp.float32) + static_pulled.astype(jnp.float32)).astype(jnp.bfloat16)

    def backward(member_pair):
        control, member = member_pair
        weighted = (member.reshape(flat_shape).astype(jnp.float32) * residual.astype(jnp.float32)).astype(jnp.bfloat16)
        member_back = jnp.dot(weighted, local_vertical, preferred_element_type=jnp.float32).astype(jnp.bfloat16).reshape(NX, NY, LEV)
        pulled_back = horizontal(member_back, local_kx[::-1], local_ky[::-1])
        return (control.astype(jnp.float32) + pulled_back.astype(jnp.float32)).astype(jnp.bfloat16)

    grad_members = lax.map(backward, (member_control, perturbations))
    return grad_static, grad_members
```

```python
import functools

import jax
import jax.numpy as jnp
from jax import lax
from jax.experimental import pallas as pl
from jax.experimental.pallas import tpu as pltpu
from jax.sharding import PartitionSpec as P

TILE = 48
SLAB = 32
BF = jnp.bfloat16
F32 = jnp.float32


VMEM = pl.BlockSpec(memory_space=pltpu.VMEM)
ANY = pl.BlockSpec(memory_space=pl.ANY)


def call(kernel, out_shape, args, flops, scratch=(), in_any=(), out_any=(), aliases=None):
    outs = tuple(out_shape)
    moved = sum(a.size * a.dtype.itemsize for a in args)
    moved += sum(o.size * jnp.dtype(o.dtype).itemsize for o in outs)
    return pl.pallas_call(
        kernel,
        out_shape=outs,
        in_specs=[ANY if i in in_any else VMEM for i in range(len(args))],
        out_specs=tuple(ANY if i in out_any else VMEM for i in range(len(outs))),
        scratch_shapes=list(scratch),
        input_output_aliases=aliases or {},
        compiler_params=pltpu.CompilerParams(vmem_limit_bytes=20 << 20),
        cost_estimate=pl.CostEstimate(flops=flops, bytes_accessed=moved, transcendentals=0),
    )(*args)


def shape(*sizes, dtype=BF):
    return jax.ShapeDtypeStruct(sizes, dtype)


def band(row, rows, cols):
    spread = jnp.broadcast_to(row, (rows, row.shape[1]))
    return pltpu.roll(spread, 0, 1, stride=1, stride_axis=0)[:, :cols].astype(BF)


def halves(a):
    return jnp.concatenate([a[: a.shape[0] // 2], a[a.shape[0] // 2 :]], axis=-1)


def unhalves(a):
    n = a.shape[-1] // 2
    return jnp.concatenate([a[..., :n], a[..., n:]], axis=0)


def dot(a, b):
    return jnp.dot(a, b, preferred_element_type=F32)


def along_y(matrix, line, count, store):
    def step(i, carry):
        pair = jnp.concatenate([line(2 * i), line(2 * i + 1)], axis=1)
        out = dot(matrix, pair)
        store(2 * i, out[:, :128])
        store(2 * i + 1, out[:, 128:])
        return carry

    lax.fori_loop(0, count // 2, step, 0, unroll=count // 2)


def along_x(matrix, parts):
    turned = [jnp.swapaxes(p, 0, 1) for p in parts]
    outs = []
    for j in range(0, 16, 2):
        cols = [
            jnp.concatenate([t[j + k] for t in turned], axis=0) if len(turned) > 1 else turned[0][j + k]
            for k in (0, 1)
        ]
        out = dot(matrix, jnp.concatenate(cols, axis=1))
        outs += [out[:, :128].astype(BF), out[:, 128:].astype(BF)]
    return jnp.swapaxes(jnp.stack(outs), 0, 1)


def static_parts(left, own, right):
    swap = jnp.concatenate([own[..., 64:], own[..., :64]], axis=-1)
    first = jnp.concatenate([unhalves(left), swap[..., 64:]], axis=-1)
    last = jnp.concatenate([swap[..., :64], unhalves(right)], axis=-1)
    return jnp.concatenate([first, own, last], axis=0)


def pack_slabs(packed, right_ref, left_ref):
    right_ref[2304:] = packed[:, 16:48].reshape(768, 128)
    left_ref[2304:] = packed[:, :SLAB].reshape(768, 128)


def take_kernel(member_ref, out_ref, sems):
    copies = [
        pltpu.make_async_copy(member_ref.at[0, pl.ds(12 * i, 12)], out_ref.at[pl.ds(12 * i, 12)], sems.at[i])
        for i in range(4)
    ]
    for copy in copies:
        copy.start()
    for copy in copies:
        copy.wait()


def pack_kernel(static_ref, member_ref, after_ref, right_ref, left_ref, own_ref, static, second, sems):
    copies = [
        pltpu.make_async_copy(member_ref.at[1, pl.ds(24 * i, 24)], second.at[pl.ds(24 * i, 24)], sems.at[i])
        for i in range(2)
    ]
    copies += [
        pltpu.make_async_copy(static_ref.at[pl.ds(24 * i, 24)], static.at[pl.ds(24 * i, 24)], sems.at[2 + i])
        for i in range(2)
    ]
    for copy in copies:
        copy.start()
    for copy in copies:
        copy.wait()
    member = second[...].reshape(2304, 128)
    right_ref[:2304] = member
    left_ref[:2304] = member
    packed = halves(static[...])
    own_ref[...] = packed
    pack_slabs(packed, right_ref, left_ref)


def first_y_kernel(row_m, row_s, taps_ref, sent_ref, own_ref, left_ref, right_ref, to_r_ref, to_l_ref, out_ref):
    member = band(taps_ref[row_m : row_m + 1], TILE, 144)
    static = band(taps_ref[row_s : row_s + 1], TILE, 112)

    def member_line(x):
        at = pl.ds(pl.multiple_of(x * TILE, TILE), TILE)
        return jnp.concatenate([left_ref[at], sent_ref[at], right_ref[at]], axis=0)

    def member_store(x, out):
        out = out.astype(BF)
        to_r_ref[x] = out
        to_l_ref[x] = out

    along_y(member, member_line, TILE, member_store)

    def static_line(x):
        at = pl.ds(pl.multiple_of(2304 + x * SLAB, SLAB), SLAB)
        return jnp.concatenate([left_ref[at], own_ref[x], right_ref[at]], axis=0)

    def static_store(x, out):
        out_ref[x] = out.astype(BF)

    along_y(static, static_line, 24, static_store)
    packed = out_ref[...]
    to_r_ref[TILE:] = halves(packed[..., 64:])
    to_l_ref[TILE:] = halves(packed[..., :64])


def first_x_kernel(row, taps_ref, own_ref, left_ref, right_ref, out_ref):
    matrix = band(taps_ref[row : row + 1], TILE, 144)
    for c in range(0, TILE, 16):
        at = slice(c, c + 16)
        out_ref[:, at] = along_x(matrix, [left_ref[:, at], own_ref[:, at], right_ref[:, at]])


def second_y(row, taps_ref, own_ref, left_ref, right_ref, store):
    matrix = band(taps_ref[row : row + 1], TILE, 144)

    def line(x):
        return jnp.concatenate([left_ref[x], own_ref[x], right_ref[x]], axis=0)

    along_y(matrix, line, TILE, store)


def second_x(rows, taps_ref, own_ref, left_ref, right_ref, s_ref, block):
    matrix = band(taps_ref[rows[0] : rows[0] + 1], TILE, 144)
    matrix_s = band(taps_ref[rows[1] : rows[1] + 1], 24, 72)
    for c in range(0, TILE, 16):
        at = slice(c, c + 16)
        b = along_x(matrix, [left_ref[:TILE, at], own_ref[:TILE, at], right_ref[:TILE, at]])
        lines = static_parts(left_ref[TILE:, at], s_ref[:, at], right_ref[TILE:, at])
        block(at, b, along_x(matrix_s, [lines]))


def static_block(static_ref):
    full = static_ref[...]
    cols = jnp.where(lax.axis_index("mem") == 0, full[:, :64], full[:, 64:])
    zero = jnp.zeros_like(cols)
    return jnp.concatenate([jnp.concatenate([cols, zero], axis=1), jnp.concatenate([zero, cols], axis=1)], axis=0)


def dot_t(a, b):
    return lax.dot_general(a, b, (((1,), (1,)), ((), ())), preferred_element_type=F32)


def forward_a_kernel(row, taps_ref, own_ref, left_ref, right_ref, pert_ref, vert_ref, out_ref, filtered):
    def store(x, out):
        filtered[x] = out.astype(BF)

    second_y(row, taps_ref, own_ref, left_ref, right_ref, store)
    vert = vert_ref[...]

    def step(i, carry):
        at = pl.ds(8 * i, 8)
        local = dot_t(filtered[at].reshape(384, 128), vert).reshape(8, TILE, 128)
        out_ref[at] = pert_ref[0, at].astype(F32) * local
        return carry

    lax.fori_loop(0, 6, step, 0, unroll=2)


def forward_b_kernel(
    rows, taps_ref, own_ref, left_ref, right_ref, s_ref, first_ref, pert_ref, vert_ref, static_ref,
    kept_ref, sent_ref
):
    vert = vert_ref[...]
    static_mat = static_block(static_ref)

    def block(at, b, s):
        total = first_ref[:, at]
        total += pert_ref[1, :, at].astype(F32) * dot_t(b.reshape(768, 128), vert).reshape(TILE, 16, 128)
        static = dot_t(s.reshape(384, 128), static_mat)
        total += jnp.concatenate([static[:, :128], static[:, 128:]], axis=0).reshape(TILE, 16, 128)
        kept_ref[:, at] = total
        sent_ref[:, at] = total.astype(BF)

    second_x(rows, taps_ref, own_ref, left_ref, right_ref, s_ref, block)


def residual_kernel(
    kept_ref, came_ref, dep_ref, weight_ref, pert_ref, vert_ref, static_ref,
    a_ref, right_ref, left_ref, own_ref
):
    vert = vert_ref[...]
    static_mat = static_block(static_ref)

    def step(i, carry):
        res = []
        for x in (4 * i, 24 + 4 * i):
            at = pl.ds(x, 4)
            total = kept_ref[at] + came_ref[at].astype(F32)
            r = (weight_ref[at].astype(F32) * (total - dep_ref[at].astype(F32))).astype(BF)
            r32 = r.astype(F32)
            res.append(r.reshape(192, 128))
            first = (pert_ref[0, at].astype(F32) * r32).astype(BF).reshape(192, 128)
            second = (pert_ref[1, at].astype(F32) * r32).astype(BF).reshape(192, 128)
            a_ref[at] = dot(first, vert).astype(BF).reshape(4, TILE, 128)
            back = dot(second, vert).astype(BF)
            cells = pl.ds(pl.multiple_of(x * TILE, 192), 192)
            right_ref[cells] = back
            left_ref[cells] = back
        static = dot(jnp.concatenate(res, axis=1), static_mat).astype(BF)
        own_ref[pl.ds(4 * i, 4)] = static.reshape(4, TILE, 128)
        return carry

    lax.fori_loop(0, 6, step, 0, unroll=2)
    pack_slabs(own_ref[...], right_ref, left_ref)


def last_a_kernel(row, taps_ref, own_ref, left_ref, right_ref, member_ref, out_ref, out, sems):
    def store(x, filtered):
        out[x] = (member_ref[0, x].astype(F32) + filtered.astype(BF).astype(F32)).astype(BF)

    second_y(row, taps_ref, own_ref, left_ref, right_ref, store)
    copies = [
        pltpu.make_async_copy(out.at[pl.ds(12 * i, 12)], out_ref.at[0, pl.ds(12 * i, 12)], sems.at[i])
        for i in range(4)
    ]
    for copy in copies:
        copy.start()
    for copy in copies:
        copy.wait()


def last_b_kernel(
    rows, taps_ref, own_ref, left_ref, right_ref, s_ref, member_ref, control_ref, begun_ref,
    static_out, member_out, static, member, sems
):
    copies = []

    def block(at, b, s):
        i = len(copies) // 2
        member[i] = (member_ref[1, :, at].astype(F32) + b.astype(F32)).astype(BF)
        both = control_ref[:, at].astype(F32) + s.astype(F32)
        static[i] = unhalves(both.astype(BF))
        for copy in (
            pltpu.make_async_copy(member.at[i], member_out.at[1, :, at], sems.at[0, i]),
            pltpu.make_async_copy(static.at[i], static_out.at[:, at], sems.at[1, i]),
        ):
            copy.start()
            copies.append(copy)

    second_x(rows, taps_ref, own_ref, left_ref, right_ref, s_ref, block)
    for copy in copies:
        copy.wait()


def from_left(field, axis):
    size = lax.axis_size(axis)
    return lax.ppermute(field, axis, [(i, i + 1) for i in range(size - 1)])


def from_right(field, axis):
    size = lax.axis_size(axis)
    return lax.ppermute(field, axis, [(i + 1, i) for i in range(size - 1)])


def first_filters(taps, back, a, to_r, to_l, own):
    a_halo = (from_left(a, "tx"), from_right(a, "tx"))
    b_halo = (from_left(to_r, "ty"), from_right(to_l, "ty"))
    tile = (TILE, TILE, 128)
    b_to_r, b_to_l, s = call(
        functools.partial(first_y_kernel, 1 + back, 3 + back),
        (shape(60, TILE, 128), shape(60, TILE, 128), shape(24, TILE, 128)),
        (taps, to_r, own) + b_halo,
        700_000_000,
    )
    b_halo = (from_left(b_to_r, "tx"), from_right(b_to_l, "tx"))
    (a,) = call(functools.partial(first_x_kernel, back), (shape(*tile),), (taps, a) + a_halo, 500_000_000)
    a_halo = (from_left(a, "ty"), from_right(a, "ty"))
    return (a,) + a_halo, (b_to_r,) + b_halo + (s,)


def body(
    static_control,
    member_control,
    perturbations,
    departures,
    obs_weight,
    static_kx,
    static_ky,
    local_kx,
    local_ky,
    static_vertical,
    local_vertical,
):
    rows = []
    for flip in (False, True):
        for taps, start in ((local_kx, 0), (local_ky, 0), (static_kx, 0), (static_ky, SLAB - 24)):
            taps = taps[::-1] if flip else taps
            rows.append(jnp.pad(taps.astype(F32), (start, 256 - start - taps.shape[0])))
    taps = jnp.stack(rows)
    tile = (TILE, TILE, 128)
    sent_shapes = (shape(3072, 128), shape(3072, 128), shape(24, TILE, 128))

    (a,) = call(
        take_kernel, (shape(*tile),), (member_control,), 1_000_000,
        [pltpu.SemaphoreType.DMA((4,))], in_any=(0,),
    )
    to_r, to_l, control = call(
        pack_kernel, sent_shapes, (static_control, member_control, a), 1_000_000,
        [pltpu.VMEM((TILE, TILE, 64), BF), pltpu.VMEM(tile, BF), pltpu.SemaphoreType.DMA((4,))],
        in_any=(0, 1, 2),
    )
    a, b = first_filters(taps, 0, a, to_r, to_l, control)
    (first,) = call(
        functools.partial(forward_a_kernel, 1), (shape(*tile, dtype=F32),),
        (taps,) + a + (perturbations, local_vertical), 800_000_000, [pltpu.VMEM(tile, BF)],
    )
    kept, sent = call(
        functools.partial(forward_b_kernel, (0, 2)), (shape(*tile, dtype=F32), shape(*tile)),
        (taps,) + b + (first, perturbations, local_vertical, static_vertical), 1_000_000_000,
    )
    size = lax.axis_size("mem")
    came = lax.ppermute(sent, "mem", [(i, size - 1 - i) for i in range(size)])
    a, to_r, to_l, own = call(
        residual_kernel, (shape(*tile),) + sent_shapes,
        (kept, came, departures, obs_weight, perturbations, local_vertical, static_vertical), 400_000_000,
    )
    a, b = first_filters(taps, 4, a, to_r, to_l, own)
    (begun,) = call(
        functools.partial(last_a_kernel, 5), (shape(2, *tile),), (taps,) + a + (member_control,), 500_000_000,
        [pltpu.VMEM(tile, BF), pltpu.SemaphoreType.DMA((4,))], out_any=(0,),
    )
    args = (taps,) + b + (member_control, control, begun)
    return tuple(call(
        functools.partial(last_b_kernel, (4, 6)), (shape(TILE, TILE, 64), shape(2, *tile)), args, 700_000_000,
        [pltpu.VMEM((3, TILE, 16, 64), BF), pltpu.VMEM((3, TILE, 16, 128), BF), pltpu.SemaphoreType.DMA((2, 3))],
        in_any=(len(args) - 1,), out_any=(0, 1), aliases={len(args) - 1: 1},
    ))


def solution(mesh):
    return jax.shard_map(
        body,
        mesh=mesh,
        in_specs=(
            P("tx", "ty", "mem"),
            P("mem", "tx", "ty", None),
            P("mem", "tx", "ty", None),
            P("tx", "ty", None),
            P("tx", "ty", None),
            P(),
            P(),
            P(),
            P(),
            P(),
            P(),
        ),
        out_specs=(P("tx", "ty", "mem"), P("mem", "tx", "ty", None)),
        check_vma=False,
    )
```

```python
import functools

import jax
import jax.numpy as jnp
from jax import lax
from jax.experimental import pallas as pl
from jax.experimental.pallas import tpu as pltpu
from jax.sharding import PartitionSpec as P

TILE = 48
SLAB = 32
BF = jnp.bfloat16
F32 = jnp.float32


VMEM = pl.BlockSpec(memory_space=pltpu.VMEM)
ANY = pl.BlockSpec(memory_space=pl.ANY)


def call(kernel, out_shape, args, flops, scratch=(), in_any=(), out_any=(), aliases=None):
    outs = tuple(out_shape)
    moved = sum(a.size * a.dtype.itemsize for a in args)
    moved += sum(o.size * jnp.dtype(o.dtype).itemsize for o in outs)
    return pl.pallas_call(
        kernel,
        out_shape=outs,
        in_specs=[ANY if i in in_any else VMEM for i in range(len(args))],
        out_specs=tuple(ANY if i in out_any else VMEM for i in range(len(outs))),
        scratch_shapes=list(scratch),
        input_output_aliases=aliases or {},
        compiler_params=pltpu.CompilerParams(vmem_limit_bytes=20 << 20),
        cost_estimate=pl.CostEstimate(flops=flops, bytes_accessed=moved, transcendentals=0),
    )(*args)


def shape(*sizes, dtype=BF):
    return jax.ShapeDtypeStruct(sizes, dtype)


def band(row, rows, cols):
    spread = jnp.broadcast_to(row, (rows, row.shape[1]))
    return pltpu.roll(spread, 0, 1, stride=1, stride_axis=0)[:, :cols].astype(BF)


def place(axis):
    at = lax.axis_index(axis)
    return at % 2 == 1, (at == 0) | (at == lax.axis_size(axis) - 1)


def band_swapped(row, axis):
    spread = jnp.broadcast_to(row, (TILE, row.shape[1]))
    plain = pltpu.roll(spread, 0, 1, stride=1, stride_axis=0)
    right = pltpu.roll(spread, row.shape[1] - 96, 1, stride=1, stride_axis=0)
    left = pltpu.roll(spread, 96, 1, stride=1, stride_axis=0)
    lane = lax.broadcasted_iota(jnp.int32, plain.shape, 1)
    odd, end = place(axis)
    turned = jnp.where(lane < 48, right, jnp.where(lane < 96, plain, left))
    both = jnp.where(jnp.full(plain.shape, odd.astype(jnp.int32)) == 1, plain, turned)
    keep = (lane < 96) | (jnp.full(plain.shape, end.astype(jnp.int32)) == 0)
    return jnp.where(keep, both, 0.0)[:, :144].astype(BF)


def pick(odd, a, b):
    return jnp.where(odd, a, b)


def sides(even, odd_swap, axis):
    odd, end = place(axis)
    outer = pick(end, jnp.zeros_like(odd_swap), odd_swap)
    return pick(odd, even, outer), pick(odd, outer, even)


def halves(a):
    return jnp.concatenate([a[: a.shape[0] // 2], a[a.shape[0] // 2 :]], axis=-1)


def unhalves(a):
    n = a.shape[-1] // 2
    return jnp.concatenate([a[..., :n], a[..., n:]], axis=0)


def dot(a, b):
    return jnp.dot(a, b, preferred_element_type=F32)


def along_y(matrix, line, count, store):
    def step(i, carry):
        pair = jnp.concatenate([line(2 * i), line(2 * i + 1)], axis=1)
        out = dot(matrix, pair)
        store(2 * i, out[:, :128])
        store(2 * i + 1, out[:, 128:])
        return carry

    lax.fori_loop(0, count // 2, step, 0, unroll=count // 2)


def along_x(matrix, parts):
    turned = [jnp.swapaxes(p, 0, 1) for p in parts]
    outs = []
    for j in range(0, 16, 2):
        cols = [
            jnp.concatenate([t[j + k] for t in turned], axis=0) if len(turned) > 1 else turned[0][j + k]
            for k in (0, 1)
        ]
        out = dot(matrix, jnp.concatenate(cols, axis=1))
        outs += [out[:, :128].astype(BF), out[:, 128:].astype(BF)]
    return jnp.swapaxes(jnp.stack(outs), 0, 1)


def static_parts(left, own, right):
    swap = jnp.concatenate([own[..., 64:], own[..., :64]], axis=-1)
    first = jnp.concatenate([unhalves(left), swap[..., 64:]], axis=-1)
    last = jnp.concatenate([swap[..., :64], unhalves(right)], axis=-1)
    return jnp.concatenate([first, own, last], axis=0)


def pack_slabs(packed, even_ref, odd_ref):
    right = packed[:, 16:48].reshape(768, 128)
    left = packed[:, :SLAB].reshape(768, 128)
    odd, _ = place("ty")
    even_ref[2304:] = pick(odd, left, right)
    odd_ref[2304:] = pick(odd, right, left)


def take_kernel(member_ref, out_ref, sems):
    copies = [
        pltpu.make_async_copy(member_ref.at[0, pl.ds(12 * i, 12)], out_ref.at[pl.ds(12 * i, 12)], sems.at[i])
        for i in range(4)
    ]
    for copy in copies:
        copy.start()
    for copy in copies:
        copy.wait()


def pack_kernel(static_ref, member_ref, after_ref, even_ref, odd_ref, own_ref, static, second, sems):
    copies = [
        pltpu.make_async_copy(member_ref.at[1, pl.ds(24 * i, 24)], second.at[pl.ds(24 * i, 24)], sems.at[i])
        for i in range(2)
    ]
    copies += [
        pltpu.make_async_copy(static_ref.at[pl.ds(24 * i, 24)], static.at[pl.ds(24 * i, 24)], sems.at[2 + i])
        for i in range(2)
    ]
    for copy in copies:
        copy.start()
    for copy in copies:
        copy.wait()
    member = second[...].reshape(2304, 128)
    even_ref[:2304] = member
    odd_ref[:2304] = member
    packed = halves(static[...])
    own_ref[...] = packed
    pack_slabs(packed, even_ref, odd_ref)


def first_y_kernel(row_m, row_s, taps_ref, sent_ref, own_ref, even_ref, odd_ref, to_even_ref, to_odd_ref, out_ref):
    member = band_swapped(taps_ref[row_m : row_m + 1], "ty")
    static = band(taps_ref[row_s : row_s + 1], TILE, 112)

    def member_line(x):
        at = pl.ds(pl.multiple_of(x * TILE, TILE), TILE)
        return jnp.concatenate([even_ref[at], sent_ref[at], odd_ref[at]], axis=0)

    def member_store(x, out):
        out = out.astype(BF)
        to_even_ref[x] = out
        to_odd_ref[x] = out

    along_y(member, member_line, TILE, member_store)

    def static_line(x):
        at = pl.ds(pl.multiple_of(2304 + x * SLAB, SLAB), SLAB)
        left, right = sides(even_ref[at], odd_ref[at], "ty")
        return jnp.concatenate([left, own_ref[x], right], axis=0)

    def static_store(x, out):
        out_ref[x] = out.astype(BF)

    along_y(static, static_line, 24, static_store)
    packed = out_ref[...]
    right = halves(packed[..., 64:])
    left = halves(packed[..., :64])
    odd, _ = place("tx")
    to_even_ref[TILE:] = pick(odd, left, right)
    to_odd_ref[TILE:] = pick(odd, right, left)


def first_x_kernel(row, taps_ref, own_ref, even_ref, odd_ref, out_ref):
    matrix = band_swapped(taps_ref[row : row + 1], "tx")
    for c in range(0, TILE, 16):
        at = slice(c, c + 16)
        out_ref[:, at] = along_x(matrix, [even_ref[:, at], own_ref[:, at], odd_ref[:, at]])


def second_y(row, taps_ref, own_ref, even_ref, odd_ref, store):
    matrix = band_swapped(taps_ref[row : row + 1], "ty")

    def line(x):
        return jnp.concatenate([even_ref[x], own_ref[x], odd_ref[x]], axis=0)

    along_y(matrix, line, TILE, store)


def second_x(rows, taps_ref, own_ref, even_ref, odd_ref, s_ref, block):
    matrix = band_swapped(taps_ref[rows[0] : rows[0] + 1], "tx")
    matrix_s = band(taps_ref[rows[1] : rows[1] + 1], 24, 72)
    for c in range(0, TILE, 16):
        at = slice(c, c + 16)
        b = along_x(matrix, [even_ref[:TILE, at], own_ref[:TILE, at], odd_ref[:TILE, at]])
        left, right = sides(even_ref[TILE:, at], odd_ref[TILE:, at], "tx")
        lines = static_parts(left, s_ref[:, at], right)
        block(at, b, along_x(matrix_s, [lines]))


def static_block(static_ref):
    full = static_ref[...]
    cols = jnp.where(lax.axis_index("mem") == 0, full[:, :64], full[:, 64:])
    zero = jnp.zeros_like(cols)
    return jnp.concatenate([jnp.concatenate([cols, zero], axis=1), jnp.concatenate([zero, cols], axis=1)], axis=0)


def dot_t(a, b):
    return lax.dot_general(a, b, (((1,), (1,)), ((), ())), preferred_element_type=F32)


def forward_a_kernel(row, taps_ref, own_ref, even_ref, odd_ref, pert_ref, vert_ref, out_ref, filtered):
    def store(x, out):
        filtered[x] = out.astype(BF)

    second_y(row, taps_ref, own_ref, even_ref, odd_ref, store)
    vert = vert_ref[...]

    def step(i, carry):
        at = pl.ds(8 * i, 8)
        local = dot_t(filtered[at].reshape(384, 128), vert).reshape(8, TILE, 128)
        out_ref[at] = pert_ref[0, at].astype(F32) * local
        return carry

    lax.fori_loop(0, 6, step, 0, unroll=2)


def forward_b_kernel(
    rows, taps_ref, own_ref, even_ref, odd_ref, s_ref, first_ref, pert_ref, vert_ref, static_ref,
    kept_ref, sent_ref
):
    vert = vert_ref[...]
    static_mat = static_block(static_ref)

    def block(at, b, s):
        total = first_ref[:, at]
        total += pert_ref[1, :, at].astype(F32) * dot_t(b.reshape(768, 128), vert).reshape(TILE, 16, 128)
        static = dot_t(s.reshape(384, 128), static_mat)
        total += jnp.concatenate([static[:, :128], static[:, 128:]], axis=0).reshape(TILE, 16, 128)
        kept_ref[:, at] = total
        sent_ref[:, at] = total.astype(BF)

    second_x(rows, taps_ref, own_ref, even_ref, odd_ref, s_ref, block)


def residual_kernel(
    kept_ref, came_ref, dep_ref, weight_ref, pert_ref, vert_ref, static_ref,
    a_ref, even_ref, odd_ref, own_ref
):
    vert = vert_ref[...]
    static_mat = static_block(static_ref)

    def step(i, carry):
        res = []
        for x in (4 * i, 24 + 4 * i):
            at = pl.ds(x, 4)
            total = kept_ref[at] + came_ref[at].astype(F32)
            r = (weight_ref[at].astype(F32) * (total - dep_ref[at].astype(F32))).astype(BF)
            r32 = r.astype(F32)
            res.append(r.reshape(192, 128))
            first = (pert_ref[0, at].astype(F32) * r32).astype(BF).reshape(192, 128)
            second = (pert_ref[1, at].astype(F32) * r32).astype(BF).reshape(192, 128)
            a_ref[at] = dot(first, vert).astype(BF).reshape(4, TILE, 128)
            back = dot(second, vert).astype(BF)
            cells = pl.ds(pl.multiple_of(x * TILE, 192), 192)
            even_ref[cells] = back
            odd_ref[cells] = back
        static = dot(jnp.concatenate(res, axis=1), static_mat).astype(BF)
        own_ref[pl.ds(4 * i, 4)] = static.reshape(4, TILE, 128)
        return carry

    lax.fori_loop(0, 6, step, 0, unroll=2)
    pack_slabs(own_ref[...], even_ref, odd_ref)


def last_a_kernel(row, taps_ref, own_ref, even_ref, odd_ref, member_ref, out_ref, out, sems):
    def store(x, filtered):
        out[x] = (member_ref[0, x].astype(F32) + filtered.astype(BF).astype(F32)).astype(BF)

    second_y(row, taps_ref, own_ref, even_ref, odd_ref, store)
    copies = [
        pltpu.make_async_copy(out.at[pl.ds(12 * i, 12)], out_ref.at[0, pl.ds(12 * i, 12)], sems.at[i])
        for i in range(4)
    ]
    for copy in copies:
        copy.start()
    for copy in copies:
        copy.wait()


def last_b_kernel(
    rows, taps_ref, own_ref, even_ref, odd_ref, s_ref, member_ref, control_ref, begun_ref,
    static_out, member_out, static, member, sems
):
    copies = []

    def block(at, b, s):
        i = len(copies) // 2
        member[i] = (member_ref[1, :, at].astype(F32) + b.astype(F32)).astype(BF)
        both = control_ref[:, at].astype(F32) + s.astype(F32)
        static[i] = unhalves(both.astype(BF))
        for copy in (
            pltpu.make_async_copy(member.at[i], member_out.at[1, :, at], sems.at[0, i]),
            pltpu.make_async_copy(static.at[i], static_out.at[:, at], sems.at[1, i]),
        ):
            copy.start()
            copies.append(copy)

    second_x(rows, taps_ref, own_ref, even_ref, odd_ref, s_ref, block)
    for copy in copies:
        copy.wait()


def swaps_y(even, odd):
    n = lax.axis_size("ty")
    first = [(i, i ^ 1) for i in range(n)]
    second = [(i, (i + 1) % n if i % 2 else (i - 1) % n) for i in range(n)]
    return lax.ppermute(even, "ty", first), lax.ppermute(odd, "ty", second)


def swaps_x(even, odd):
    n, m = lax.axis_size("tx"), lax.axis_size("ty")
    first = [(i, i ^ 1) for i in range(n)]
    second = []
    for i in range(n):
        other = i + 1 if i % 2 else i - 1
        for j in range(m):
            second.append((i * m + j, i * m + (j ^ 1) if i in (0, n - 1) else other * m + j))
    return lax.ppermute(even, "tx", first), lax.ppermute(odd, ("tx", "ty"), second)


def first_filters(taps, back, a, to_even, to_odd, own):
    a_halo = swaps_x(a, a)
    b_halo = swaps_y(to_even, to_odd)
    tile = (TILE, TILE, 128)
    b_to_even, b_to_odd, s = call(
        functools.partial(first_y_kernel, 1 + back, 3 + back),
        (shape(60, TILE, 128), shape(60, TILE, 128), shape(24, TILE, 128)),
        (taps, to_even, own) + b_halo,
        700_000_000,
    )
    b_halo = swaps_x(b_to_even, b_to_odd)
    (a,) = call(functools.partial(first_x_kernel, back), (shape(*tile),), (taps, a) + a_halo, 500_000_000)
    a_halo = swaps_y(a, a)
    return (a,) + a_halo, (b_to_even,) + b_halo + (s,)


def body(
    static_control,
    member_control,
    perturbations,
    departures,
    obs_weight,
    static_kx,
    static_ky,
    local_kx,
    local_ky,
    static_vertical,
    local_vertical,
):
    rows = []
    for flip in (False, True):
        for taps, start in ((local_kx, 0), (local_ky, 0), (static_kx, 0), (static_ky, SLAB - 24)):
            taps = taps[::-1] if flip else taps
            rows.append(jnp.pad(taps.astype(F32), (start, 256 - start - taps.shape[0])))
    taps = jnp.stack(rows)
    tile = (TILE, TILE, 128)
    sent_shapes = (shape(3072, 128), shape(3072, 128), shape(24, TILE, 128))

    (a,) = call(
        take_kernel, (shape(*tile),), (member_control,), 1_000_000,
        [pltpu.SemaphoreType.DMA((4,))], in_any=(0,),
    )
    to_even, to_odd, control = call(
        pack_kernel, sent_shapes, (static_control, member_control, a), 1_000_000,
        [pltpu.VMEM((TILE, TILE, 64), BF), pltpu.VMEM(tile, BF), pltpu.SemaphoreType.DMA((4,))],
        in_any=(0, 1, 2),
    )
    a, b = first_filters(taps, 0, a, to_even, to_odd, control)
    (first,) = call(
        functools.partial(forward_a_kernel, 1), (shape(*tile, dtype=F32),),
        (taps,) + a + (perturbations, local_vertical), 800_000_000, [pltpu.VMEM(tile, BF)],
    )
    kept, sent = call(
        functools.partial(forward_b_kernel, (0, 2)), (shape(*tile, dtype=F32), shape(*tile)),
        (taps,) + b + (first, perturbations, local_vertical, static_vertical), 1_000_000_000,
    )
    size = lax.axis_size("mem")
    came = lax.ppermute(sent, "mem", [(i, size - 1 - i) for i in range(size)])
    a, to_even, to_odd, own = call(
        residual_kernel, (shape(*tile),) + sent_shapes,
        (kept, came, departures, obs_weight, perturbations, local_vertical, static_vertical), 400_000_000,
    )
    a, b = first_filters(taps, 4, a, to_even, to_odd, own)
    (begun,) = call(
        functools.partial(last_a_kernel, 5), (shape(2, *tile),), (taps,) + a + (member_control,), 500_000_000,
        [pltpu.VMEM(tile, BF), pltpu.SemaphoreType.DMA((4,))], out_any=(0,),
    )
    args = (taps,) + b + (member_control, control, begun)
    return tuple(call(
        functools.partial(last_b_kernel, (4, 6)), (shape(TILE, TILE, 64), shape(2, *tile)), args, 700_000_000,
        [pltpu.VMEM((3, TILE, 16, 64), BF), pltpu.VMEM((3, TILE, 16, 128), BF), pltpu.SemaphoreType.DMA((2, 3))],
        in_any=(len(args) - 1,), out_any=(0, 1), aliases={len(args) - 1: 1},
    ))


def solution(mesh):
    return jax.shard_map(
        body,
        mesh=mesh,
        in_specs=(
            P("tx", "ty", "mem"),
            P("mem", "tx", "ty", None),
            P("mem", "tx", "ty", None),
            P("tx", "ty", None),
            P("tx", "ty", None),
            P(),
            P(),
            P(),
            P(),
            P(),
            P(),
        ),
        out_specs=(P("tx", "ty", "mem"), P("mem", "tx", "ty", None)),
        check_vma=False,
    )
```

```python
import functools

import jax
import jax.numpy as jnp
from jax import lax
from jax.experimental import pallas as pl
from jax.experimental.pallas import tpu as pltpu
from jax.sharding import PartitionSpec as P

TILE = 48
SLAB = 32
BRIEF = 1_000
LONG = 20_000_000_000
BF = jnp.bfloat16
F32 = jnp.float32


VMEM = pl.BlockSpec(memory_space=pltpu.VMEM)
ANY = pl.BlockSpec(memory_space=pl.ANY)


def call(kernel, out_shape, args, flops, scratch=(), in_any=(), out_any=(), aliases=None):
    outs = tuple(out_shape)
    moved = sum(a.size * a.dtype.itemsize for a in args)
    moved += sum(o.size * jnp.dtype(o.dtype).itemsize for o in outs)
    return pl.pallas_call(
        kernel,
        out_shape=outs,
        in_specs=[ANY if i in in_any else VMEM for i in range(len(args))],
        out_specs=tuple(ANY if i in out_any else VMEM for i in range(len(outs))),
        scratch_shapes=list(scratch),
        input_output_aliases=aliases or {},
        compiler_params=pltpu.CompilerParams(vmem_limit_bytes=20 << 20),
        cost_estimate=pl.CostEstimate(flops=flops, bytes_accessed=min(moved, flops), transcendentals=0),
    )(*args)


def shape(*sizes, dtype=BF):
    return jax.ShapeDtypeStruct(sizes, dtype)


def band(row, rows, cols):
    spread = jnp.broadcast_to(row, (rows, row.shape[1]))
    return pltpu.roll(spread, 0, 1, stride=1, stride_axis=0)[:, :cols].astype(BF)


def place(axis):
    at = lax.axis_index(axis)
    return at % 2 == 1, (at == 0) | (at == lax.axis_size(axis) - 1)


def band_swapped(row, axis):
    spread = jnp.broadcast_to(row, (TILE, row.shape[1]))
    plain = pltpu.roll(spread, 0, 1, stride=1, stride_axis=0)
    right = pltpu.roll(spread, row.shape[1] - 96, 1, stride=1, stride_axis=0)
    left = pltpu.roll(spread, 96, 1, stride=1, stride_axis=0)
    lane = lax.broadcasted_iota(jnp.int32, plain.shape, 1)
    odd, end = place(axis)
    turned = jnp.where(lane < 48, right, jnp.where(lane < 96, plain, left))
    both = jnp.where(jnp.full(plain.shape, odd.astype(jnp.int32)) == 1, plain, turned)
    keep = (lane < 96) | (jnp.full(plain.shape, end.astype(jnp.int32)) == 0)
    return jnp.where(keep, both, 0.0)[:, :144].astype(BF)


def pick(odd, a, b):
    return jnp.where(odd, a, b)


def sides(even, odd_swap, axis):
    odd, end = place(axis)
    outer = pick(end, jnp.zeros_like(odd_swap), odd_swap)
    return pick(odd, even, outer), pick(odd, outer, even)


def halves(a):
    return jnp.concatenate([a[: a.shape[0] // 2], a[a.shape[0] // 2 :]], axis=-1)


def unhalves(a):
    n = a.shape[-1] // 2
    return jnp.concatenate([a[..., :n], a[..., n:]], axis=0)


def dot(a, b):
    return jnp.dot(a, b, preferred_element_type=F32)


def along_y(matrix, line, count, store):
    def step(i, carry):
        pair = jnp.concatenate([line(2 * i), line(2 * i + 1)], axis=1)
        out = dot(matrix, pair)
        store(2 * i, out[:, :128])
        store(2 * i + 1, out[:, 128:])
        return carry

    lax.fori_loop(0, count // 2, step, 0, unroll=count // 2)


def along_x(matrix, parts):
    turned = [jnp.swapaxes(p, 0, 1) for p in parts]
    outs = []
    for j in range(0, 16, 2):
        cols = [
            jnp.concatenate([t[j + k] for t in turned], axis=0) if len(turned) > 1 else turned[0][j + k]
            for k in (0, 1)
        ]
        out = dot(matrix, jnp.concatenate(cols, axis=1))
        outs += [out[:, :128].astype(BF), out[:, 128:].astype(BF)]
    return jnp.swapaxes(jnp.stack(outs), 0, 1)


def static_parts(left, own, right):
    swap = jnp.concatenate([own[..., 64:], own[..., :64]], axis=-1)
    first = jnp.concatenate([unhalves(left), swap[..., 64:]], axis=-1)
    last = jnp.concatenate([swap[..., :64], unhalves(right)], axis=-1)
    return jnp.concatenate([first, own, last], axis=0)


def taps_kernel(lx_ref, ly_ref, sx_ref, sy_ref, out_ref):
    sub = lax.broadcasted_iota(jnp.int32, (256, 256), 0)
    lane = lax.broadcasted_iota(jnp.int32, (256, 256), 1)
    for i, (ref, start) in enumerate(((lx_ref, 0), (ly_ref, 0), (sx_ref, 0), (sy_ref, SLAB - 24))):
        n = ref.shape[0]
        taps = jnp.broadcast_to(ref[...].astype(F32)[None, :], (8, n)).astype(BF)
        for row, source in ((i, lane - start), (i + 4, n - 1 - lane + start)):
            spread = jnp.where(sub[:n] == source[:n], 1.0, 0.0).astype(BF)
            out_ref[row : row + 1] = dot(taps, spread)[:1]


def pack_slabs(packed, even_ref, odd_ref):
    right = packed[:, 16:48].reshape(768, 128)
    left = packed[:, :SLAB].reshape(768, 128)
    odd, _ = place("ty")
    even_ref[2304:] = pick(odd, left, right)
    odd_ref[2304:] = pick(odd, right, left)


def pack_x(packed, even_ref, odd_ref):
    right = halves(packed[..., 64:])
    left = halves(packed[..., :64])
    odd, _ = place("tx")
    even_ref[TILE:] = pick(odd, left, right)
    odd_ref[TILE:] = pick(odd, right, left)


def pack_kernel(member_ref, static_ref, first_ref, even_ref, odd_ref, own_ref, static, sems):
    copies = [
        pltpu.make_async_copy(static_ref.at[pl.ds(12 * i, 12)], static.at[pl.ds(12 * i, 12)], sems.at[i])
        for i in range(4)
    ]
    for copy in copies:
        copy.start()
    first_ref[...] = member_ref[0]
    second = member_ref[1].reshape(2304, 128)
    even_ref[:2304] = second
    odd_ref[:2304] = second
    for copy in copies:
        copy.wait()
    packed = halves(static[...])
    own_ref[...] = packed
    pack_slabs(packed, even_ref, odd_ref)


def first_y_kernel(row_m, row_s, taps_ref, sent_ref, own_ref, even_ref, odd_ref, to_even_ref, to_odd_ref, out_ref):
    member = band_swapped(taps_ref[row_m : row_m + 1], "ty")
    static = band(taps_ref[row_s : row_s + 1], TILE, 112)

    def member_line(x):
        at = pl.ds(pl.multiple_of(x * TILE, TILE), TILE)
        return jnp.concatenate([even_ref[at], sent_ref[at], odd_ref[at]], axis=0)

    def member_store(x, out):
        out = out.astype(BF)
        to_even_ref[x] = out
        to_odd_ref[x] = out

    along_y(member, member_line, TILE, member_store)

    def static_line(x):
        at = pl.ds(pl.multiple_of(2304 + x * SLAB, SLAB), SLAB)
        left, right = sides(even_ref[at], odd_ref[at], "ty")
        return jnp.concatenate([left, own_ref[x], right], axis=0)

    def static_store(x, out):
        out_ref[x] = out.astype(BF)

    along_y(static, static_line, 24, static_store)
    pack_x(out_ref[...], to_even_ref, to_odd_ref)


def first_x_kernel(row, taps_ref, own_ref, even_ref, odd_ref, out_ref):
    matrix = band_swapped(taps_ref[row : row + 1], "tx")
    for c in range(0, TILE, 16):
        at = slice(c, c + 16)
        out_ref[:, at] = along_x(matrix, [even_ref[:, at], own_ref[:, at], odd_ref[:, at]])


def second_y(row, taps_ref, own_ref, even_ref, odd_ref, store):
    matrix = band_swapped(taps_ref[row : row + 1], "ty")

    def line(x):
        return jnp.concatenate([even_ref[x], own_ref[x], odd_ref[x]], axis=0)

    along_y(matrix, line, TILE, store)


def second_x(rows, taps_ref, own_ref, even_ref, odd_ref, s_ref, block):
    matrix = band_swapped(taps_ref[rows[0] : rows[0] + 1], "tx")
    matrix_s = band(taps_ref[rows[1] : rows[1] + 1], 24, 72)
    for c in range(0, TILE, 16):
        at = slice(c, c + 16)
        b = along_x(matrix, [even_ref[:TILE, at], own_ref[:TILE, at], odd_ref[:TILE, at]])
        left, right = sides(even_ref[TILE:, at], odd_ref[TILE:, at], "tx")
        lines = static_parts(left, s_ref[:, at], right)
        block(at, b, along_x(matrix_s, [lines]))


def static_block(static_ref):
    full = static_ref[...]
    cols = jnp.where(lax.axis_index("mem") == 0, full[:, :64], full[:, 64:])
    zero = jnp.zeros_like(cols)
    return jnp.concatenate([jnp.concatenate([cols, zero], axis=1), jnp.concatenate([zero, cols], axis=1)], axis=0)


def dot_t(a, b):
    return lax.dot_general(a, b, (((1,), (1,)), ((), ())), preferred_element_type=F32)


def forward_a_kernel(row, taps_ref, own_ref, even_ref, odd_ref, pert_ref, vert_ref, out_ref, filtered):
    def store(x, out):
        filtered[x] = out.astype(BF)

    second_y(row, taps_ref, own_ref, even_ref, odd_ref, store)
    vert = vert_ref[...]

    def step(i, carry):
        at = pl.ds(8 * i, 8)
        local = dot_t(filtered[at].reshape(384, 128), vert).reshape(8, TILE, 128)
        out_ref[at] = pert_ref[0, at].astype(F32) * local
        return carry

    lax.fori_loop(0, 6, step, 0, unroll=2)


def forward_b_kernel(
    rows, taps_ref, own_ref, even_ref, odd_ref, s_ref, first_ref, pert_ref, vert_ref, static_ref,
    kept_ref, sent_ref
):
    vert = vert_ref[...]
    static_mat = static_block(static_ref)

    def block(at, b, s):
        total = first_ref[:, at]
        total += pert_ref[1, :, at].astype(F32) * dot_t(b.reshape(768, 128), vert).reshape(TILE, 16, 128)
        static = dot_t(s.reshape(384, 128), static_mat)
        total += jnp.concatenate([static[:, :128], static[:, 128:]], axis=0).reshape(TILE, 16, 128)
        kept_ref[:, at] = total
        sent_ref[:, at] = total.astype(BF)

    second_x(rows, taps_ref, own_ref, even_ref, odd_ref, s_ref, block)


def residual_kernel(
    kept_ref, came_ref, dep_ref, weight_ref, pert_ref, vert_ref, static_ref, even_ref, odd_ref, own_ref, b_ref
):
    vert = vert_ref[...]
    static_mat = static_block(static_ref)

    def step(i, carry):
        res = []
        for x in (4 * i, 24 + 4 * i):
            at = pl.ds(x, 4)
            total = kept_ref[at] + came_ref[at].astype(F32)
            r = (weight_ref[at].astype(F32) * (total - dep_ref[at].astype(F32))).astype(BF)
            r32 = r.astype(F32)
            res.append(r.reshape(192, 128))
            first = (pert_ref[0, at].astype(F32) * r32).astype(BF).reshape(192, 128)
            second = (pert_ref[1, at].astype(F32) * r32).astype(BF).reshape(192, 128)
            back = dot(first, vert).astype(BF).reshape(4, TILE, 128)
            even_ref[at] = back
            odd_ref[at] = back
            b_ref[at] = dot(second, vert).astype(BF).reshape(4, TILE, 128)
        static = dot(jnp.concatenate(res, axis=1), static_mat).astype(BF)
        own_ref[pl.ds(4 * i, 4)] = static.reshape(4, TILE, 128)
        return carry

    lax.fori_loop(0, 6, step, 0, unroll=2)
    pack_x(own_ref[...], even_ref, odd_ref)


def back_x_kernel(
    rows, taps_ref, sent_ref, own_ref, even_ref, odd_ref, after_ref, to_even_ref, to_odd_ref, out_ref
):
    member = band_swapped(taps_ref[rows[0] : rows[0] + 1], "tx")
    static = band(taps_ref[rows[1] : rows[1] + 1], 24, 72)
    for c in range(0, TILE, 16):
        at = slice(c, c + 16)
        out = along_x(member, [even_ref[:TILE, at], sent_ref[:TILE, at], odd_ref[:TILE, at]])
        to_even_ref[:TILE, at] = out
        to_odd_ref[:TILE, at] = out
        left, right = sides(even_ref[TILE:, at], odd_ref[TILE:, at], "tx")
        out_ref[:, at] = along_x(static, [static_parts(left, own_ref[:, at], right)])
    packed = out_ref[...]
    right = packed[:, 16:48].reshape(16, TILE, 128)
    left = packed[:, :SLAB].reshape(16, TILE, 128)
    odd, _ = place("ty")
    to_even_ref[TILE:] = pick(odd, left, right)
    to_odd_ref[TILE:] = pick(odd, right, left)


def back_y_kernel(row, taps_ref, own_ref, even_ref, odd_ref, out_ref):
    def store(x, out):
        out_ref[x] = out.astype(BF)

    second_y(row, taps_ref, own_ref, even_ref, odd_ref, store)


def last_b_kernel(row, taps_ref, own_ref, even_ref, odd_ref, member_ref, member_out, member, sems):
    matrix = band_swapped(taps_ref[row : row + 1], "tx")
    copies = []
    for i in range(3):
        at = slice(16 * i, 16 * i + 16)
        b = along_x(matrix, [even_ref[:, at], own_ref[:, at], odd_ref[:, at]])
        member[i] = (member_ref[1, :, at].astype(F32) + b.astype(F32)).astype(BF)
        copies.append(pltpu.make_async_copy(member.at[i], member_out.at[1, :, at], sems.at[i]))
        copies[i].start()
    for copy in copies:
        copy.wait()


def last_a_kernel(
    rows, taps_ref, own_ref, even_ref, odd_ref, s_ref, member_ref, control_ref, begun_ref,
    static_out, member_out, static, member, sems
):
    def store(x, out):
        member[x] = (member_ref[0, x].astype(F32) + out.astype(BF).astype(F32)).astype(BF)

    second_y(rows[0], taps_ref, own_ref, even_ref, odd_ref, store)
    copies = [
        pltpu.make_async_copy(member.at[pl.ds(24 * i, 24)], member_out.at[0, pl.ds(24 * i, 24)], sems.at[i])
        for i in range(2)
    ]
    for copy in copies:
        copy.start()
    matrix = band(taps_ref[rows[1] : rows[1] + 1], TILE, 112)
    slabs = [r[TILE:].reshape(24, SLAB, 128) for r in (even_ref, odd_ref)]
    left, right = sides(slabs[0], slabs[1], "ty")
    for x in range(0, 24, 2):
        lines = [jnp.concatenate([left[k], s_ref[k], right[k]], axis=0) for k in (x, x + 1)]
        out = dot(matrix, jnp.concatenate(lines, axis=1)).astype(BF).astype(F32)
        for k in (0, 1):
            both = (control_ref[x + k].astype(F32) + out[:, 128 * k : 128 * k + 128]).astype(BF)
            static[x + k] = both[:, :64]
            static[x + k + 24] = both[:, 64:]
    copies.append(pltpu.make_async_copy(static, static_out, sems.at[2]))
    copies[2].start()
    for copy in copies:
        copy.wait()


def swaps_y(even, odd):
    n = lax.axis_size("ty")
    first = [(i, i ^ 1) for i in range(n)]
    second = [(i, (i + 1) % n if i % 2 else (i - 1) % n) for i in range(n)]
    return lax.ppermute(even, "ty", first), lax.ppermute(odd, "ty", second)


def swaps_x(even, odd):
    n, m = lax.axis_size("tx"), lax.axis_size("ty")
    first = [(i, i ^ 1) for i in range(n)]
    second = []
    for i in range(n):
        other = i + 1 if i % 2 else i - 1
        for j in range(m):
            second.append((i * m + j, i * m + (j ^ 1) if i in (0, n - 1) else other * m + j))
    return lax.ppermute(even, "tx", first), lax.ppermute(odd, ("tx", "ty"), second)


def first_filters(taps, a, to_even, to_odd, own):
    a_halo = swaps_x(a, a)
    b_halo = swaps_y(to_even, to_odd)
    tile = (TILE, TILE, 128)
    b_to_even, b_to_odd, s = call(
        functools.partial(first_y_kernel, 1, 3),
        (shape(60, TILE, 128), shape(60, TILE, 128), shape(24, TILE, 128)),
        (taps, to_even, own) + b_halo,
        700_000_000,
    )
    b_halo = swaps_x(b_to_even, b_to_odd)
    (a,) = call(functools.partial(first_x_kernel, 0), (shape(*tile),), (taps, a) + a_halo, 500_000_000)
    a_halo = swaps_y(a, a)
    return (a,) + a_halo, (b_to_even,) + b_halo + (s,)


def body(
    static_control,
    member_control,
    perturbations,
    departures,
    obs_weight,
    static_kx,
    static_ky,
    local_kx,
    local_ky,
    static_vertical,
    local_vertical,
):
    (taps,) = call(
        taps_kernel, (shape(8, 256, dtype=F32),), (local_kx, local_ky, static_kx, static_ky), BRIEF
    )
    tile = (TILE, TILE, 128)
    sent_shapes = (shape(3072, 128), shape(3072, 128), shape(24, TILE, 128))

    a, to_even, to_odd, control = call(
        pack_kernel, (shape(*tile),) + sent_shapes, (member_control, static_control), 1_000_000,
        [pltpu.VMEM((TILE, TILE, 64), BF), pltpu.SemaphoreType.DMA((4,))], in_any=(1,),
    )
    a, b = first_filters(taps, a, to_even, to_odd, control)
    (first,) = call(
        functools.partial(forward_a_kernel, 1), (shape(*tile, dtype=F32),),
        (taps,) + a + (perturbations, local_vertical), 800_000_000, [pltpu.VMEM(tile, BF)],
    )
    kept, sent = call(
        functools.partial(forward_b_kernel, (0, 2)), (shape(*tile, dtype=F32), shape(*tile)),
        (taps,) + b + (first, perturbations, local_vertical, static_vertical), 1_000_000_000,
    )
    size = lax.axis_size("mem")
    came = lax.ppermute(sent, "mem", [(i, size - 1 - i) for i in range(size)])

    to_even, to_odd, own, b = call(
        residual_kernel, (shape(60, TILE, 128), shape(60, TILE, 128), shape(24, TILE, 128), shape(*tile)),
        (kept, came, departures, obs_weight, perturbations, local_vertical, static_vertical), 400_000_000,
    )
    a = (to_even, own) + swaps_x(to_even, to_odd)
    (b,) = call(functools.partial(back_y_kernel, 5), (shape(*tile),), (taps, b) + swaps_y(b, b), BRIEF)
    b_halo = swaps_x(b, b)
    args = (taps,) + a + (b,)
    to_even, to_odd, s = call(
        functools.partial(back_x_kernel, (4, 6)),
        (shape(64, TILE, 128), shape(64, TILE, 128), shape(24, TILE, 128)), args, LONG, in_any=(len(args) - 1,),
    )
    a = (to_even,) + swaps_y(to_even, to_odd) + (s,)
    (begun,) = call(
        functools.partial(last_b_kernel, 4), (shape(2, *tile),), (taps, b) + b_halo + (member_control,), LONG,
        [pltpu.VMEM((3, TILE, 16, 128), BF), pltpu.SemaphoreType.DMA((3,))], out_any=(0,),
    )
    args = (taps,) + a + (member_control, control, begun)
    return tuple(call(
        functools.partial(last_a_kernel, (5, 7)), (shape(TILE, TILE, 64), shape(2, *tile)), args, 700_000_000,
        [pltpu.VMEM((TILE, TILE, 64), BF), pltpu.VMEM(tile, BF), pltpu.SemaphoreType.DMA((3,))],
        in_any=(len(args) - 1,), out_any=(0, 1), aliases={len(args) - 1: 1},
    ))


def solution(mesh):
    return jax.shard_map(
        body,
        mesh=mesh,
        in_specs=(
            P("tx", "ty", "mem"),
            P("mem", "tx", "ty", None),
            P("mem", "tx", "ty", None),
            P("tx", "ty", None),
            P("tx", "ty", None),
            P(),
            P(),
            P(),
            P(),
            P(),
            P(),
        ),
        out_specs=(P("tx", "ty", "mem"), P("mem", "tx", "ty", None)),
        check_vma=False,
    )
```

```python
import functools

import jax
import jax.numpy as jnp
from jax import lax
from jax.experimental import pallas as pl
from jax.experimental.pallas import tpu as pltpu
from jax.sharding import PartitionSpec as P

TILE = 48
SLAB = 32
BRIEF = 1_000
LONG = 20_000_000_000
BF = jnp.bfloat16
F32 = jnp.float32


VMEM = pl.BlockSpec(memory_space=pltpu.VMEM)
ANY = pl.BlockSpec(memory_space=pl.ANY)


def call(kernel, out_shape, args, flops, scratch=(), in_any=(), out_any=(), aliases=None):
    outs = tuple(out_shape)
    moved = sum(a.size * a.dtype.itemsize for a in args)
    moved += sum(o.size * jnp.dtype(o.dtype).itemsize for o in outs)
    return pl.pallas_call(
        kernel,
        out_shape=outs,
        in_specs=[ANY if i in in_any else VMEM for i in range(len(args))],
        out_specs=tuple(ANY if i in out_any else VMEM for i in range(len(outs))),
        scratch_shapes=list(scratch),
        input_output_aliases=aliases or {},
        compiler_params=pltpu.CompilerParams(vmem_limit_bytes=20 << 20),
        cost_estimate=pl.CostEstimate(flops=flops, bytes_accessed=min(moved, flops), transcendentals=0),
    )(*args)


def shape(*sizes, dtype=BF):
    return jax.ShapeDtypeStruct(sizes, dtype)


def band(row, rows, cols):
    spread = jnp.broadcast_to(row, (rows, row.shape[1]))
    return pltpu.roll(spread, 0, 1, stride=1, stride_axis=0)[:, :cols].astype(BF)


def place(axis):
    at = lax.axis_index(axis)
    return at % 2 == 1, (at == 0) | (at == lax.axis_size(axis) - 1)


def band_swapped(row, axis):
    spread = jnp.broadcast_to(row, (TILE, row.shape[1]))
    plain = pltpu.roll(spread, 0, 1, stride=1, stride_axis=0)
    right = pltpu.roll(spread, row.shape[1] - 96, 1, stride=1, stride_axis=0)
    left = pltpu.roll(spread, 96, 1, stride=1, stride_axis=0)
    lane = lax.broadcasted_iota(jnp.int32, plain.shape, 1)
    odd, end = place(axis)
    turned = jnp.where(lane < 48, right, jnp.where(lane < 96, plain, left))
    both = jnp.where(jnp.full(plain.shape, odd.astype(jnp.int32)) == 1, plain, turned)
    keep = (lane < 96) | (jnp.full(plain.shape, end.astype(jnp.int32)) == 0)
    return jnp.where(keep, both, 0.0)[:, :144].astype(BF)


def pick(odd, a, b):
    return jnp.where(odd, a, b)


def sides(even, odd_swap, axis):
    odd, end = place(axis)
    outer = pick(end, jnp.zeros_like(odd_swap), odd_swap)
    return pick(odd, even, outer), pick(odd, outer, even)


def halves(a):
    return jnp.concatenate([a[: a.shape[0] // 2], a[a.shape[0] // 2 :]], axis=-1)


def unhalves(a):
    n = a.shape[-1] // 2
    return jnp.concatenate([a[..., :n], a[..., n:]], axis=0)


def dot(a, b):
    return jnp.dot(a, b, preferred_element_type=F32)


def along_y(matrix, line, count, store):
    def step(i, carry):
        pair = jnp.concatenate([line(2 * i), line(2 * i + 1)], axis=1)
        out = dot(matrix, pair)
        store(2 * i, out[:, :128])
        store(2 * i + 1, out[:, 128:])
        return carry

    lax.fori_loop(0, count // 2, step, 0, unroll=count // 2)


def along_x(matrix, parts):
    turned = [jnp.swapaxes(p, 0, 1) for p in parts]
    outs = []
    for j in range(0, 16, 2):
        cols = [
            jnp.concatenate([t[j + k] for t in turned], axis=0) if len(turned) > 1 else turned[0][j + k]
            for k in (0, 1)
        ]
        out = dot(matrix, jnp.concatenate(cols, axis=1))
        outs += [out[:, :128].astype(BF), out[:, 128:].astype(BF)]
    return jnp.swapaxes(jnp.stack(outs), 0, 1)


def static_parts(left, own, right):
    swap = jnp.concatenate([own[..., 64:], own[..., :64]], axis=-1)
    first = jnp.concatenate([unhalves(left), swap[..., 64:]], axis=-1)
    last = jnp.concatenate([swap[..., :64], unhalves(right)], axis=-1)
    return jnp.concatenate([first, own, last], axis=0)


def taps_kernel(lx_ref, ly_ref, sx_ref, sy_ref, out_ref):
    sub = lax.broadcasted_iota(jnp.int32, (256, 256), 0)
    lane = lax.broadcasted_iota(jnp.int32, (256, 256), 1)
    for i, (ref, start) in enumerate(((lx_ref, 0), (ly_ref, 0), (sx_ref, 0), (sy_ref, SLAB - 24))):
        n = ref.shape[0]
        taps = jnp.broadcast_to(ref[...].astype(F32)[None, :], (8, n)).astype(BF)
        for row, source in ((i, lane - start), (i + 4, n - 1 - lane + start)):
            spread = jnp.where(sub[:n] == source[:n], 1.0, 0.0).astype(BF)
            out_ref[row : row + 1] = dot(taps, spread)[:1]


def pack_slabs(packed, even_ref, odd_ref):
    right = packed[:, 16:48].reshape(768, 128)
    left = packed[:, :SLAB].reshape(768, 128)
    odd, _ = place("ty")
    even_ref[2304:] = pick(odd, left, right)
    odd_ref[2304:] = pick(odd, right, left)


def pack_x(packed, even_ref, odd_ref):
    right = halves(packed[..., 64:])
    left = halves(packed[..., :64])
    odd, _ = place("tx")
    even_ref[TILE:] = pick(odd, left, right)
    odd_ref[TILE:] = pick(odd, right, left)


def pack_kernel(member_ref, static_ref, first_ref, even_ref, odd_ref, own_ref):
    first_ref[...] = member_ref[0]
    second = member_ref[1].reshape(2304, 128)
    even_ref[:2304] = second
    odd_ref[:2304] = second
    packed = halves(static_ref[...])
    own_ref[...] = packed
    pack_slabs(packed, even_ref, odd_ref)


def first_y_kernel(row_m, row_s, taps_ref, sent_ref, own_ref, even_ref, odd_ref, to_even_ref, to_odd_ref, out_ref):
    member = band_swapped(taps_ref[row_m : row_m + 1], "ty")
    static = band(taps_ref[row_s : row_s + 1], TILE, 112)

    def member_line(x):
        at = pl.ds(pl.multiple_of(x * TILE, TILE), TILE)
        return jnp.concatenate([even_ref[at], sent_ref[at], odd_ref[at]], axis=0)

    def member_store(x, out):
        out = out.astype(BF)
        to_even_ref[x] = out
        to_odd_ref[x] = out

    along_y(member, member_line, TILE, member_store)

    def static_line(x):
        at = pl.ds(pl.multiple_of(2304 + x * SLAB, SLAB), SLAB)
        left, right = sides(even_ref[at], odd_ref[at], "ty")
        return jnp.concatenate([left, own_ref[x], right], axis=0)

    def static_store(x, out):
        out_ref[x] = out.astype(BF)

    along_y(static, static_line, 24, static_store)
    pack_x(out_ref[...], to_even_ref, to_odd_ref)


def first_x_kernel(row, taps_ref, own_ref, even_ref, odd_ref, out_ref):
    matrix = band_swapped(taps_ref[row : row + 1], "tx")
    for c in range(0, TILE, 16):
        at = slice(c, c + 16)
        out_ref[:, at] = along_x(matrix, [even_ref[:, at], own_ref[:, at], odd_ref[:, at]])


def second_y(row, taps_ref, own_ref, even_ref, odd_ref, store):
    matrix = band_swapped(taps_ref[row : row + 1], "ty")

    def line(x):
        return jnp.concatenate([even_ref[x], own_ref[x], odd_ref[x]], axis=0)

    along_y(matrix, line, TILE, store)


def second_x(rows, taps_ref, own_ref, even_ref, odd_ref, s_ref, block):
    matrix = band_swapped(taps_ref[rows[0] : rows[0] + 1], "tx")
    matrix_s = band(taps_ref[rows[1] : rows[1] + 1], 24, 72)
    for c in range(0, TILE, 16):
        at = slice(c, c + 16)
        b = along_x(matrix, [even_ref[:TILE, at], own_ref[:TILE, at], odd_ref[:TILE, at]])
        left, right = sides(even_ref[TILE:, at], odd_ref[TILE:, at], "tx")
        lines = static_parts(left, s_ref[:, at], right)
        block(at, b, along_x(matrix_s, [lines]))


def static_block(static_ref):
    full = static_ref[...]
    cols = jnp.where(lax.axis_index("mem") == 0, full[:, :64], full[:, 64:])
    zero = jnp.zeros_like(cols)
    return jnp.concatenate([jnp.concatenate([cols, zero], axis=1), jnp.concatenate([zero, cols], axis=1)], axis=0)


def dot_t(a, b):
    return lax.dot_general(a, b, (((1,), (1,)), ((), ())), preferred_element_type=F32)


def forward_a_kernel(row, taps_ref, own_ref, even_ref, odd_ref, pert_ref, vert_ref, out_ref, filtered):
    def store(x, out):
        filtered[x] = out.astype(BF)

    second_y(row, taps_ref, own_ref, even_ref, odd_ref, store)
    vert = vert_ref[...]

    def step(i, carry):
        at = pl.ds(8 * i, 8)
        local = dot_t(filtered[at].reshape(384, 128), vert).reshape(8, TILE, 128)
        out_ref[at] = pert_ref[0, at].astype(F32) * local
        return carry

    lax.fori_loop(0, 6, step, 0, unroll=2)


def forward_b_kernel(
    rows, taps_ref, own_ref, even_ref, odd_ref, s_ref, first_ref, pert_ref, vert_ref, static_ref,
    kept_ref, sent_ref
):
    vert = vert_ref[...]
    static_mat = static_block(static_ref)

    def block(at, b, s):
        total = first_ref[:, at]
        total += pert_ref[1, :, at].astype(F32) * dot_t(b.reshape(768, 128), vert).reshape(TILE, 16, 128)
        static = dot_t(s.reshape(384, 128), static_mat)
        total += jnp.concatenate([static[:, :128], static[:, 128:]], axis=0).reshape(TILE, 16, 128)
        kept_ref[:, at] = total
        sent_ref[:, at] = total.astype(BF)

    second_x(rows, taps_ref, own_ref, even_ref, odd_ref, s_ref, block)


def residual_kernel(
    kept_ref, came_ref, dep_ref, weight_ref, pert_ref, vert_ref, static_ref, even_ref, odd_ref, own_ref, b_ref
):
    vert = vert_ref[...]
    static_mat = static_block(static_ref)

    def step(i, carry):
        res = []
        for x in (4 * i, 24 + 4 * i):
            at = pl.ds(x, 4)
            total = kept_ref[at] + came_ref[at].astype(F32)
            r = (weight_ref[at].astype(F32) * (total - dep_ref[at].astype(F32))).astype(BF)
            r32 = r.astype(F32)
            res.append(r.reshape(192, 128))
            first = (pert_ref[0, at].astype(F32) * r32).astype(BF).reshape(192, 128)
            second = (pert_ref[1, at].astype(F32) * r32).astype(BF).reshape(192, 128)
            back = dot(first, vert).astype(BF).reshape(4, TILE, 128)
            even_ref[at] = back
            odd_ref[at] = back
            b_ref[at] = dot(second, vert).astype(BF).reshape(4, TILE, 128)
        static = dot(jnp.concatenate(res, axis=1), static_mat).astype(BF)
        own_ref[pl.ds(4 * i, 4)] = static.reshape(4, TILE, 128)
        return carry

    lax.fori_loop(0, 6, step, 0, unroll=2)
    pack_x(own_ref[...], even_ref, odd_ref)


def back_x_kernel(
    rows, taps_ref, sent_ref, own_ref, even_ref, odd_ref, after_ref, to_even_ref, to_odd_ref, out_ref
):
    member = band_swapped(taps_ref[rows[0] : rows[0] + 1], "tx")
    static = band(taps_ref[rows[1] : rows[1] + 1], 24, 72)
    for c in range(0, TILE, 16):
        at = slice(c, c + 16)
        out = along_x(member, [even_ref[:TILE, at], sent_ref[:TILE, at], odd_ref[:TILE, at]])
        to_even_ref[:TILE, at] = out
        to_odd_ref[:TILE, at] = out
        left, right = sides(even_ref[TILE:, at], odd_ref[TILE:, at], "tx")
        out_ref[:, at] = along_x(static, [static_parts(left, own_ref[:, at], right)])
    packed = out_ref[...]
    right = packed[:, 16:48].reshape(16, TILE, 128)
    left = packed[:, :SLAB].reshape(16, TILE, 128)
    odd, _ = place("ty")
    to_even_ref[TILE:] = pick(odd, left, right)
    to_odd_ref[TILE:] = pick(odd, right, left)


def back_y_kernel(row, taps_ref, own_ref, even_ref, odd_ref, out_ref):
    def store(x, out):
        out_ref[x] = out.astype(BF)

    second_y(row, taps_ref, own_ref, even_ref, odd_ref, store)


def last_b_kernel(row, taps_ref, own_ref, even_ref, odd_ref, member_ref, member_out, member, sems):
    matrix = band_swapped(taps_ref[row : row + 1], "tx")
    copies = []
    for i in range(3):
        at = slice(16 * i, 16 * i + 16)
        b = along_x(matrix, [even_ref[:, at], own_ref[:, at], odd_ref[:, at]])
        member[i] = (member_ref[1, :, at].astype(F32) + b.astype(F32)).astype(BF)
        copies.append(pltpu.make_async_copy(member.at[i], member_out.at[1, :, at], sems.at[i]))
        copies[i].start()
    for copy in copies:
        copy.wait()


def last_a_kernel(
    rows, taps_ref, own_ref, even_ref, odd_ref, s_ref, member_ref, control_ref, begun_ref,
    static_out, member_out, static, member, sems
):
    copies = []

    def send(source, target):
        copies.append(pltpu.make_async_copy(source, target, sems.at[len(copies)]))
        copies[-1].start()

    matrix = band(taps_ref[rows[1] : rows[1] + 1], TILE, 112)
    slabs = [r[TILE:].reshape(24, SLAB, 128) for r in (even_ref, odd_ref)]
    left, right = sides(slabs[0], slabs[1], "ty")
    for x in range(0, 24, 2):
        lines = [jnp.concatenate([left[k], s_ref[k], right[k]], axis=0) for k in (x, x + 1)]
        out = dot(matrix, jnp.concatenate(lines, axis=1)).astype(BF).astype(F32)
        for k in (0, 1):
            both = (control_ref[x + k].astype(F32) + out[:, 128 * k : 128 * k + 128]).astype(BF)
            static[x + k] = both[:, :64]
            static[x + k + 24] = both[:, 64:]
        if x % 12 == 10:
            for part in (pl.ds(x - 10, 12), pl.ds(x + 14, 12)):
                send(static.at[part], static_out.at[part])
    matrix = band_swapped(taps_ref[rows[0] : rows[0] + 1], "ty")
    for first in range(0, TILE, 12):

        def line(x):
            x = first + x
            return jnp.concatenate([even_ref[x], own_ref[x], odd_ref[x]], axis=0)

        def store(x, out):
            x = first + x
            member[x] = (member_ref[0, x].astype(F32) + out.astype(BF).astype(F32)).astype(BF)

        along_y(matrix, line, 12, store)
        part = pl.ds(first, 12)
        send(member.at[part], member_out.at[0, part])
    for copy in copies:
        copy.wait()


def swaps_y(even, odd):
    n = lax.axis_size("ty")
    first = [(i, i ^ 1) for i in range(n)]
    second = [(i, (i + 1) % n if i % 2 else (i - 1) % n) for i in range(n)]
    return lax.ppermute(even, "ty", first), lax.ppermute(odd, "ty", second)


def swaps_x(even, odd):
    n, m = lax.axis_size("tx"), lax.axis_size("ty")
    first = [(i, i ^ 1) for i in range(n)]
    second = []
    for i in range(n):
        other = i + 1 if i % 2 else i - 1
        for j in range(m):
            second.append((i * m + j, i * m + (j ^ 1) if i in (0, n - 1) else other * m + j))
    return lax.ppermute(even, "tx", first), lax.ppermute(odd, ("tx", "ty"), second)


def first_filters(taps, a, to_even, to_odd, own):
    a_halo = swaps_x(a, a)
    b_halo = swaps_y(to_even, to_odd)
    tile = (TILE, TILE, 128)
    b_to_even, b_to_odd, s = call(
        functools.partial(first_y_kernel, 1, 3),
        (shape(60, TILE, 128), shape(60, TILE, 128), shape(24, TILE, 128)),
        (taps, to_even, own) + b_halo,
        700_000_000,
    )
    b_halo = swaps_x(b_to_even, b_to_odd)
    (a,) = call(functools.partial(first_x_kernel, 0), (shape(*tile),), (taps, a) + a_halo, 500_000_000)
    a_halo = swaps_y(a, a)
    return (a,) + a_halo, (b_to_even,) + b_halo + (s,)


def body(
    static_control,
    member_control,
    perturbations,
    departures,
    obs_weight,
    static_kx,
    static_ky,
    local_kx,
    local_ky,
    static_vertical,
    local_vertical,
):
    (taps,) = call(
        taps_kernel, (shape(8, 256, dtype=F32),), (local_kx, local_ky, static_kx, static_ky), BRIEF
    )
    tile = (TILE, TILE, 128)
    sent_shapes = (shape(3072, 128), shape(3072, 128), shape(24, TILE, 128))

    a, to_even, to_odd, control = call(
        pack_kernel, (shape(*tile),) + sent_shapes, (member_control, static_control), 1_000_000
    )
    a, b = first_filters(taps, a, to_even, to_odd, control)
    (first,) = call(
        functools.partial(forward_a_kernel, 1), (shape(*tile, dtype=F32),),
        (taps,) + a + (perturbations, local_vertical), 800_000_000, [pltpu.VMEM(tile, BF)],
    )
    kept, sent = call(
        functools.partial(forward_b_kernel, (0, 2)), (shape(*tile, dtype=F32), shape(*tile)),
        (taps,) + b + (first, perturbations, local_vertical, static_vertical), 1_000_000_000,
    )
    size = lax.axis_size("mem")
    came = lax.ppermute(sent, "mem", [(i, size - 1 - i) for i in range(size)])

    to_even, to_odd, own, b = call(
        residual_kernel, (shape(60, TILE, 128), shape(60, TILE, 128), shape(24, TILE, 128), shape(*tile)),
        (kept, came, departures, obs_weight, perturbations, local_vertical, static_vertical), 400_000_000,
    )
    a = (to_even, own) + swaps_x(to_even, to_odd)
    (b,) = call(functools.partial(back_y_kernel, 5), (shape(*tile),), (taps, b) + swaps_y(b, b), BRIEF)
    b_halo = swaps_x(b, b)
    args = (taps,) + a + (b,)
    to_even, to_odd, s = call(
        functools.partial(back_x_kernel, (4, 6)),
        (shape(64, TILE, 128), shape(64, TILE, 128), shape(24, TILE, 128)), args, LONG, in_any=(len(args) - 1,),
    )
    a = (to_even,) + swaps_y(to_even, to_odd) + (s,)
    (begun,) = call(
        functools.partial(last_b_kernel, 4), (shape(2, *tile),), (taps, b) + b_halo + (member_control,), LONG,
        [pltpu.VMEM((3, TILE, 16, 128), BF), pltpu.SemaphoreType.DMA((3,))], out_any=(0,),
    )
    args = (taps,) + a + (member_control, control, begun)
    return tuple(call(
        functools.partial(last_a_kernel, (5, 7)), (shape(TILE, TILE, 64), shape(2, *tile)), args, 700_000_000,
        [pltpu.VMEM((TILE, TILE, 64), BF), pltpu.VMEM(tile, BF), pltpu.SemaphoreType.DMA((8,))],
        in_any=(len(args) - 1,), out_any=(0, 1), aliases={len(args) - 1: 1},
    ))


def solution(mesh):
    return jax.shard_map(
        body,
        mesh=mesh,
        in_specs=(
            P("tx", "ty", "mem"),
            P("mem", "tx", "ty", None),
            P("mem", "tx", "ty", None),
            P("tx", "ty", None),
            P("tx", "ty", None),
            P(),
            P(),
            P(),
            P(),
            P(),
            P(),
        ),
        out_specs=(P("tx", "ty", "mem"), P("mem", "tx", "ty", None)),
        check_vma=False,
    )
```

```python
import functools

import jax
import jax.numpy as jnp
from jax import lax
from jax.experimental import pallas as pl
from jax.experimental.pallas import tpu as pltpu
from jax.sharding import PartitionSpec as P

TILE = 48
SLAB = 32
BRIEF = 1_000
LONG = 20_000_000_000
BF = jnp.bfloat16
F32 = jnp.float32


VMEM = pl.BlockSpec(memory_space=pltpu.VMEM)
ANY = pl.BlockSpec(memory_space=pl.ANY)


def call(kernel, out_shape, args, flops, scratch=(), in_any=(), out_any=(), aliases=None):
    outs = tuple(out_shape)
    moved = sum(a.size * a.dtype.itemsize for a in args)
    moved += sum(o.size * jnp.dtype(o.dtype).itemsize for o in outs)
    return pl.pallas_call(
        kernel,
        out_shape=outs,
        in_specs=[ANY if i in in_any else VMEM for i in range(len(args))],
        out_specs=tuple(ANY if i in out_any else VMEM for i in range(len(outs))),
        scratch_shapes=list(scratch),
        input_output_aliases=aliases or {},
        compiler_params=pltpu.CompilerParams(vmem_limit_bytes=20 << 20),
        cost_estimate=pl.CostEstimate(flops=flops, bytes_accessed=min(moved, flops), transcendentals=0),
    )(*args)


def shape(*sizes, dtype=BF):
    return jax.ShapeDtypeStruct(sizes, dtype)


def band(row, rows, cols):
    spread = jnp.broadcast_to(row, (rows, row.shape[1]))
    return pltpu.roll(spread, 0, 1, stride=1, stride_axis=0)[:, :cols].astype(BF)


def place(axis):
    at = lax.axis_index(axis)
    return at % 2 == 1, (at == 0) | (at == lax.axis_size(axis) - 1)


def band_swapped(row, axis):
    spread = jnp.broadcast_to(row, (TILE, row.shape[1]))
    plain = pltpu.roll(spread, 0, 1, stride=1, stride_axis=0)
    right = pltpu.roll(spread, row.shape[1] - 96, 1, stride=1, stride_axis=0)
    left = pltpu.roll(spread, 96, 1, stride=1, stride_axis=0)
    lane = lax.broadcasted_iota(jnp.int32, plain.shape, 1)
    odd, end = place(axis)
    turned = jnp.where(lane < 48, right, jnp.where(lane < 96, plain, left))
    both = jnp.where(jnp.full(plain.shape, odd.astype(jnp.int32)) == 1, plain, turned)
    keep = (lane < 96) | (jnp.full(plain.shape, end.astype(jnp.int32)) == 0)
    return jnp.where(keep, both, 0.0)[:, :144].astype(BF)


def pick(odd, a, b):
    return jnp.where(odd, a, b)


def sides(even, odd_swap, axis):
    odd, end = place(axis)
    outer = pick(end, jnp.zeros_like(odd_swap), odd_swap)
    return pick(odd, even, outer), pick(odd, outer, even)


def halves(a):
    return jnp.concatenate([a[: a.shape[0] // 2], a[a.shape[0] // 2 :]], axis=-1)


def unhalves(a):
    n = a.shape[-1] // 2
    return jnp.concatenate([a[..., :n], a[..., n:]], axis=0)


def dot(a, b):
    return jnp.dot(a, b, preferred_element_type=F32)


def along_y(matrix, line, count, store):
    def step(i, carry):
        pair = jnp.concatenate([line(2 * i), line(2 * i + 1)], axis=1)
        out = dot(matrix, pair)
        store(2 * i, out[:, :128])
        store(2 * i + 1, out[:, 128:])
        return carry

    lax.fori_loop(0, count // 2, step, 0, unroll=count // 2)


def along_x(matrix, parts):
    turned = [jnp.swapaxes(p, 0, 1) for p in parts]
    outs = []
    for j in range(0, 16, 2):
        cols = [
            jnp.concatenate([t[j + k] for t in turned], axis=0) if len(turned) > 1 else turned[0][j + k]
            for k in (0, 1)
        ]
        out = dot(matrix, jnp.concatenate(cols, axis=1))
        outs += [out[:, :128].astype(BF), out[:, 128:].astype(BF)]
    return jnp.swapaxes(jnp.stack(outs), 0, 1)


def static_parts(left, own, right):
    swap = jnp.concatenate([own[..., 64:], own[..., :64]], axis=-1)
    first = jnp.concatenate([unhalves(left), swap[..., 64:]], axis=-1)
    last = jnp.concatenate([swap[..., :64], unhalves(right)], axis=-1)
    return jnp.concatenate([first, own, last], axis=0)


def taps_kernel(lx_ref, ly_ref, sx_ref, sy_ref, out_ref):
    sub = lax.broadcasted_iota(jnp.int32, (256, 256), 0)
    lane = lax.broadcasted_iota(jnp.int32, (256, 256), 1)
    for i, (ref, start) in enumerate(((lx_ref, 0), (ly_ref, 0), (sx_ref, 0), (sy_ref, SLAB - 24))):
        n = ref.shape[0]
        taps = jnp.broadcast_to(ref[...].astype(F32)[None, :], (8, n)).astype(BF)
        for row, source in ((i, lane - start), (i + 4, n - 1 - lane + start)):
            spread = jnp.where(sub[:n] == source[:n], 1.0, 0.0).astype(BF)
            out_ref[row : row + 1] = dot(taps, spread)[:1]


def pack_slabs(packed, even_ref, odd_ref):
    right = packed[:, 16:48].reshape(768, 128)
    left = packed[:, :SLAB].reshape(768, 128)
    odd, _ = place("ty")
    even_ref[2304:] = pick(odd, left, right)
    odd_ref[2304:] = pick(odd, right, left)


def pack_x(packed, even_ref, odd_ref):
    right = halves(packed[..., 64:])
    left = halves(packed[..., :64])
    odd, _ = place("tx")
    even_ref[TILE:] = pick(odd, left, right)
    odd_ref[TILE:] = pick(odd, right, left)


def pack_kernel(member_ref, static_ref, first_ref, even_ref, odd_ref, own_ref):
    first_ref[...] = member_ref[0]
    second = member_ref[1].reshape(2304, 128)
    even_ref[:2304] = second
    odd_ref[:2304] = second
    packed = halves(static_ref[...])
    own_ref[...] = packed
    pack_slabs(packed, even_ref, odd_ref)


def first_y_kernel(row_m, row_s, taps_ref, sent_ref, own_ref, even_ref, odd_ref, to_even_ref, to_odd_ref, out_ref):
    member = band_swapped(taps_ref[row_m : row_m + 1], "ty")
    static = band(taps_ref[row_s : row_s + 1], TILE, 112)

    def member_line(x):
        at = pl.ds(pl.multiple_of(x * TILE, TILE), TILE)
        return jnp.concatenate([even_ref[at], sent_ref[at], odd_ref[at]], axis=0)

    def member_store(x, out):
        out = out.astype(BF)
        to_even_ref[x] = out
        to_odd_ref[x] = out

    along_y(member, member_line, TILE, member_store)

    def static_line(x):
        at = pl.ds(pl.multiple_of(2304 + x * SLAB, SLAB), SLAB)
        left, right = sides(even_ref[at], odd_ref[at], "ty")
        return jnp.concatenate([left, own_ref[x], right], axis=0)

    def static_store(x, out):
        out_ref[x] = out.astype(BF)

    along_y(static, static_line, 24, static_store)
    pack_x(out_ref[...], to_even_ref, to_odd_ref)


def first_x_kernel(row, taps_ref, own_ref, even_ref, odd_ref, out_ref):
    matrix = band_swapped(taps_ref[row : row + 1], "tx")
    for c in range(0, TILE, 16):
        at = slice(c, c + 16)
        out_ref[:, at] = along_x(matrix, [even_ref[:, at], own_ref[:, at], odd_ref[:, at]])


def second_y(row, taps_ref, own_ref, even_ref, odd_ref, store):
    matrix = band_swapped(taps_ref[row : row + 1], "ty")

    def line(x):
        return jnp.concatenate([even_ref[x], own_ref[x], odd_ref[x]], axis=0)

    along_y(matrix, line, TILE, store)


def second_x(rows, taps_ref, own_ref, even_ref, odd_ref, s_ref, block):
    matrix = band_swapped(taps_ref[rows[0] : rows[0] + 1], "tx")
    matrix_s = band(taps_ref[rows[1] : rows[1] + 1], 24, 72)
    for c in range(0, TILE, 16):
        at = slice(c, c + 16)
        b = along_x(matrix, [even_ref[:TILE, at], own_ref[:TILE, at], odd_ref[:TILE, at]])
        left, right = sides(even_ref[TILE:, at], odd_ref[TILE:, at], "tx")
        lines = static_parts(left, s_ref[:, at], right)
        block(at, b, along_x(matrix_s, [lines]))


def static_block(static_ref):
    full = static_ref[...]
    cols = jnp.where(lax.axis_index("mem") == 0, full[:, :64], full[:, 64:])
    zero = jnp.zeros_like(cols)
    return jnp.concatenate([jnp.concatenate([cols, zero], axis=1), jnp.concatenate([zero, cols], axis=1)], axis=0)


def dot_t(a, b):
    return lax.dot_general(a, b, (((1,), (1,)), ((), ())), preferred_element_type=F32)


def forward_a_kernel(row, taps_ref, own_ref, even_ref, odd_ref, pert_ref, vert_ref, out_ref, filtered):
    def store(x, out):
        filtered[x] = out.astype(BF)

    second_y(row, taps_ref, own_ref, even_ref, odd_ref, store)
    vert = vert_ref[...]

    def step(i, carry):
        at = pl.ds(8 * i, 8)
        local = dot_t(filtered[at].reshape(384, 128), vert).reshape(8, TILE, 128)
        out_ref[at] = pert_ref[0, at].astype(F32) * local
        return carry

    lax.fori_loop(0, 6, step, 0, unroll=6)


def forward_b_kernel(
    rows, taps_ref, own_ref, even_ref, odd_ref, s_ref, first_ref, pert_ref, vert_ref, static_ref,
    kept_ref, sent_ref
):
    vert = vert_ref[...]
    static_mat = static_block(static_ref)

    def block(at, b, s):
        total = first_ref[:, at]
        total += pert_ref[1, :, at].astype(F32) * dot_t(b.reshape(768, 128), vert).reshape(TILE, 16, 128)
        static = dot_t(s.reshape(384, 128), static_mat)
        total += jnp.concatenate([static[:, :128], static[:, 128:]], axis=0).reshape(TILE, 16, 128)
        kept_ref[:, at] = total
        sent_ref[:, at] = total.astype(BF)

    second_x(rows, taps_ref, own_ref, even_ref, odd_ref, s_ref, block)


def residual_kernel(
    kept_ref, came_ref, dep_ref, weight_ref, pert_ref, vert_ref, static_ref, even_ref, odd_ref, own_ref, b_ref
):
    vert = vert_ref[...]
    static_mat = static_block(static_ref)

    def step(i, carry):
        res = []
        for x in (4 * i, 24 + 4 * i):
            at = pl.ds(x, 4)
            total = kept_ref[at] + came_ref[at].astype(F32)
            r = (weight_ref[at].astype(F32) * (total - dep_ref[at].astype(F32))).astype(BF)
            r32 = r.astype(F32)
            res.append(r.reshape(192, 128))
            first = (pert_ref[0, at].astype(F32) * r32).astype(BF).reshape(192, 128)
            second = (pert_ref[1, at].astype(F32) * r32).astype(BF).reshape(192, 128)
            back = dot(first, vert).astype(BF).reshape(4, TILE, 128)
            even_ref[at] = back
            odd_ref[at] = back
            b_ref[at] = dot(second, vert).astype(BF).reshape(4, TILE, 128)
        static = dot(jnp.concatenate(res, axis=1), static_mat).astype(BF)
        own_ref[pl.ds(4 * i, 4)] = static.reshape(4, TILE, 128)
        return carry

    lax.fori_loop(0, 6, step, 0, unroll=6)
    pack_x(own_ref[...], even_ref, odd_ref)


def back_x_kernel(
    rows, taps_ref, sent_ref, own_ref, even_ref, odd_ref, after_ref, to_even_ref, to_odd_ref, slab_ref, out_ref
):
    member = band_swapped(taps_ref[rows[0] : rows[0] + 1], "tx")
    static = band(taps_ref[rows[1] : rows[1] + 1], 24, 72)
    for c in range(0, TILE, 16):
        at = slice(c, c + 16)
        out = along_x(member, [even_ref[:TILE, at], sent_ref[:TILE, at], odd_ref[:TILE, at]])
        to_even_ref[:TILE, at] = out
        to_odd_ref[:, at] = out
        left, right = sides(even_ref[TILE:, at], odd_ref[TILE:, at], "tx")
        out_ref[:, at] = along_x(static, [static_parts(left, own_ref[:, at], right)])
    packed = out_ref[...]
    right = packed[:, 16:48].reshape(16, TILE, 128)
    left = packed[:, :SLAB].reshape(16, TILE, 128)
    odd, _ = place("ty")
    to_even_ref[TILE:] = pick(odd, left, right)
    slab_ref[...] = pick(odd, right, left)


def back_y_kernel(row, taps_ref, own_ref, even_ref, odd_ref, out_ref):
    def store(x, out):
        out_ref[x] = out.astype(BF)

    second_y(row, taps_ref, own_ref, even_ref, odd_ref, store)


def last_b_kernel(row, taps_ref, own_ref, even_ref, odd_ref, member_ref, member_out, member, sems):
    matrix = band_swapped(taps_ref[row : row + 1], "tx")
    copies = []
    for i in range(3):
        at = slice(16 * i, 16 * i + 16)
        b = along_x(matrix, [even_ref[:, at], own_ref[:, at], odd_ref[:, at]])
        member[i] = (member_ref[1, :, at].astype(F32) + b.astype(F32)).astype(BF)
        copies.append(pltpu.make_async_copy(member.at[i], member_out.at[1, :, at], sems.at[i]))
        copies[i].start()
    for copy in copies:
        copy.wait()


def last_a_kernel(
    rows, taps_ref, own_ref, even_ref, odd_ref, slab_ref, s_ref, member_ref, control_ref, begun_ref,
    static_out, member_out, static, member, sems
):
    copies = []

    def send(source, target):
        copies.append(pltpu.make_async_copy(source, target, sems.at[len(copies)]))
        copies[-1].start()

    matrix = band(taps_ref[rows[1] : rows[1] + 1], TILE, 112)
    slabs = [r.reshape(24, SLAB, 128) for r in (even_ref[TILE:], slab_ref[...])]
    left, right = sides(slabs[0], slabs[1], "ty")
    for x in range(0, 24, 2):
        lines = [jnp.concatenate([left[k], s_ref[k], right[k]], axis=0) for k in (x, x + 1)]
        out = dot(matrix, jnp.concatenate(lines, axis=1)).astype(BF).astype(F32)
        for k in (0, 1):
            both = (control_ref[x + k].astype(F32) + out[:, 128 * k : 128 * k + 128]).astype(BF)
            static[x + k] = both[:, :64]
            static[x + k + 24] = both[:, 64:]
        if x % 12 == 10:
            for part in (pl.ds(x - 10, 12), pl.ds(x + 14, 12)):
                send(static.at[part], static_out.at[part])
    matrix = band_swapped(taps_ref[rows[0] : rows[0] + 1], "ty")
    for first in range(0, TILE, 12):

        def line(x):
            x = first + x
            return jnp.concatenate([even_ref[x], own_ref[x], odd_ref[x]], axis=0)

        def store(x, out):
            x = first + x
            member[x] = (member_ref[0, x].astype(F32) + out.astype(BF).astype(F32)).astype(BF)

        along_y(matrix, line, 12, store)
        part = pl.ds(first, 12)
        send(member.at[part], member_out.at[0, part])
    for copy in copies:
        copy.wait()


def swaps_y(even, *odd):
    n = lax.axis_size("ty")
    first = [(i, i ^ 1) for i in range(n)]
    second = [(i, (i + 1) % n if i % 2 else (i - 1) % n) for i in range(n)]
    return (lax.ppermute(even, "ty", first),) + tuple(lax.ppermute(part, "ty", second) for part in odd)


def swaps_x(even, odd):
    n, m = lax.axis_size("tx"), lax.axis_size("ty")
    first = [(i, i ^ 1) for i in range(n)]
    second = []
    for i in range(n):
        other = i + 1 if i % 2 else i - 1
        for j in range(m):
            second.append((i * m + j, i * m + (j ^ 1) if i in (0, n - 1) else other * m + j))
    return lax.ppermute(even, "tx", first), lax.ppermute(odd, ("tx", "ty"), second)


def first_filters(taps, a, to_even, to_odd, own):
    a_halo = swaps_x(a, a)
    b_halo = swaps_y(to_even, to_odd)
    tile = (TILE, TILE, 128)
    b_to_even, b_to_odd, s = call(
        functools.partial(first_y_kernel, 1, 3),
        (shape(60, TILE, 128), shape(60, TILE, 128), shape(24, TILE, 128)),
        (taps, to_even, own) + b_halo,
        700_000_000,
    )
    b_halo = swaps_x(b_to_even, b_to_odd)
    (a,) = call(functools.partial(first_x_kernel, 0), (shape(*tile),), (taps, a) + a_halo, 500_000_000)
    a_halo = swaps_y(a, a)
    return (a,) + a_halo, (b_to_even,) + b_halo + (s,)


def body(
    static_control,
    member_control,
    perturbations,
    departures,
    obs_weight,
    static_kx,
    static_ky,
    local_kx,
    local_ky,
    static_vertical,
    local_vertical,
):
    (taps,) = call(
        taps_kernel, (shape(8, 256, dtype=F32),), (local_kx, local_ky, static_kx, static_ky), BRIEF
    )
    tile = (TILE, TILE, 128)
    sent_shapes = (shape(3072, 128), shape(3072, 128), shape(24, TILE, 128))

    a, to_even, to_odd, control = call(
        pack_kernel, (shape(*tile),) + sent_shapes, (member_control, static_control), 1_000_000
    )
    a, b = first_filters(taps, a, to_even, to_odd, control)
    (first,) = call(
        functools.partial(forward_a_kernel, 1), (shape(*tile, dtype=F32),),
        (taps,) + a + (perturbations, local_vertical), 800_000_000, [pltpu.VMEM(tile, BF)],
    )
    kept, sent = call(
        functools.partial(forward_b_kernel, (0, 2)), (shape(*tile, dtype=F32), shape(*tile)),
        (taps,) + b + (first, perturbations, local_vertical, static_vertical), 1_000_000_000,
    )
    size = lax.axis_size("mem")
    came = lax.ppermute(sent, "mem", [(i, size - 1 - i) for i in range(size)])

    to_even, to_odd, own, b = call(
        residual_kernel, (shape(60, TILE, 128), shape(60, TILE, 128), shape(24, TILE, 128), shape(*tile)),
        (kept, came, departures, obs_weight, perturbations, local_vertical, static_vertical), 400_000_000,
    )
    a = (to_even, own) + swaps_x(to_even, to_odd)
    (b,) = call(functools.partial(back_y_kernel, 5), (shape(*tile),), (taps, b) + swaps_y(b, b), BRIEF)
    b_halo = swaps_x(b, b)
    args = (taps,) + a + (b,)
    to_even, to_odd, slab, s = call(
        functools.partial(back_x_kernel, (4, 6)),
        (shape(64, TILE, 128), shape(*tile), shape(16, TILE, 128), shape(24, TILE, 128)), args, LONG,
        in_any=(len(args) - 1,),
    )
    a = (to_even,) + swaps_y(to_even, to_odd, slab) + (s,)
    (begun,) = call(
        functools.partial(last_b_kernel, 4), (shape(2, *tile),), (taps, b) + b_halo + (member_control,), LONG,
        [pltpu.VMEM((3, TILE, 16, 128), BF), pltpu.SemaphoreType.DMA((3,))], out_any=(0,),
    )
    args = (taps,) + a + (member_control, control, begun)
    return tuple(call(
        functools.partial(last_a_kernel, (5, 7)), (shape(TILE, TILE, 64), shape(2, *tile)), args, 700_000_000,
        [pltpu.VMEM((TILE, TILE, 64), BF), pltpu.VMEM(tile, BF), pltpu.SemaphoreType.DMA((8,))],
        in_any=(len(args) - 1,), out_any=(0, 1), aliases={len(args) - 1: 1},
    ))


def solution(mesh):
    return jax.shard_map(
        body,
        mesh=mesh,
        in_specs=(
            P("tx", "ty", "mem"),
            P("mem", "tx", "ty", None),
            P("mem", "tx", "ty", None),
            P("tx", "ty", None),
            P("tx", "ty", None),
            P(),
            P(),
            P(),
            P(),
            P(),
            P(),
        ),
        out_specs=(P("tx", "ty", "mem"), P("mem", "tx", "ty", None)),
        check_vma=False,
    )
```

```python
import functools

import jax
import jax.numpy as jnp
from jax import lax
from jax.experimental import pallas as pl
from jax.experimental.pallas import tpu as pltpu
from jax.sharding import PartitionSpec as P

TILE = 48
SLAB = 32
BRIEF = 1_000
LONG = 20_000_000_000
BF = jnp.bfloat16
F32 = jnp.float32


VMEM = pl.BlockSpec(memory_space=pltpu.VMEM)
ANY = pl.BlockSpec(memory_space=pl.ANY)


def call(kernel, out_shape, args, flops, scratch=(), in_any=(), out_any=(), aliases=None):
    outs = tuple(out_shape)
    moved = sum(a.size * a.dtype.itemsize for a in args)
    moved += sum(o.size * jnp.dtype(o.dtype).itemsize for o in outs)
    return pl.pallas_call(
        kernel,
        out_shape=outs,
        in_specs=[ANY if i in in_any else VMEM for i in range(len(args))],
        out_specs=tuple(ANY if i in out_any else VMEM for i in range(len(outs))),
        scratch_shapes=list(scratch),
        input_output_aliases=aliases or {},
        compiler_params=pltpu.CompilerParams(vmem_limit_bytes=20 << 20),
        cost_estimate=pl.CostEstimate(flops=flops, bytes_accessed=min(moved, flops), transcendentals=0),
    )(*args)


def shape(*sizes, dtype=BF):
    return jax.ShapeDtypeStruct(sizes, dtype)


def band(row, rows, cols):
    spread = jnp.broadcast_to(row, (rows, row.shape[1]))
    return pltpu.roll(spread, 0, 1, stride=1, stride_axis=0)[:, :cols].astype(BF)


def place(axis):
    at = lax.axis_index(axis)
    return at % 2 == 1, (at == 0) | (at == lax.axis_size(axis) - 1)


def band_swapped(row, axis):
    spread = jnp.broadcast_to(row, (TILE, row.shape[1]))
    plain = pltpu.roll(spread, 0, 1, stride=1, stride_axis=0)
    right = pltpu.roll(spread, row.shape[1] - 96, 1, stride=1, stride_axis=0)
    left = pltpu.roll(spread, 96, 1, stride=1, stride_axis=0)
    lane = lax.broadcasted_iota(jnp.int32, plain.shape, 1)
    odd, end = place(axis)
    turned = jnp.where(lane < 48, right, jnp.where(lane < 96, plain, left))
    both = jnp.where(jnp.full(plain.shape, odd.astype(jnp.int32)) == 1, plain, turned)
    keep = (lane < 96) | (jnp.full(plain.shape, end.astype(jnp.int32)) == 0)
    return jnp.where(keep, both, 0.0)[:, :144].astype(BF)


def pick(odd, a, b):
    return jnp.where(odd, a, b)


def sides(even, odd_swap, axis):
    odd, end = place(axis)
    outer = pick(end, jnp.zeros_like(odd_swap), odd_swap)
    return pick(odd, even, outer), pick(odd, outer, even)


def halves(a):
    return jnp.concatenate([a[: a.shape[0] // 2], a[a.shape[0] // 2 :]], axis=-1)


def unhalves(a):
    n = a.shape[-1] // 2
    return jnp.concatenate([a[..., :n], a[..., n:]], axis=0)


def dot(a, b):
    return jnp.dot(a, b, preferred_element_type=F32)


def along_y(matrix, line, count, store):
    def step(i, carry):
        pair = jnp.concatenate([line(2 * i), line(2 * i + 1)], axis=1)
        out = dot(matrix, pair)
        store(2 * i, out[:, :128])
        store(2 * i + 1, out[:, 128:])
        return carry

    lax.fori_loop(0, count // 2, step, 0, unroll=count // 2)


def along_x(matrix, parts):
    turned = [jnp.swapaxes(p, 0, 1) for p in parts]
    outs = []
    for j in range(0, 16, 2):
        cols = [
            jnp.concatenate([t[j + k] for t in turned], axis=0) if len(turned) > 1 else turned[0][j + k]
            for k in (0, 1)
        ]
        out = dot(matrix, jnp.concatenate(cols, axis=1))
        outs += [out[:, :128].astype(BF), out[:, 128:].astype(BF)]
    return jnp.swapaxes(jnp.stack(outs), 0, 1)


def static_parts(left, own, right):
    swap = jnp.concatenate([own[..., 64:], own[..., :64]], axis=-1)
    first = jnp.concatenate([unhalves(left), swap[..., 64:]], axis=-1)
    last = jnp.concatenate([swap[..., :64], unhalves(right)], axis=-1)
    return jnp.concatenate([first, own, last], axis=0)


def taps_kernel(lx_ref, ly_ref, sx_ref, sy_ref, out_ref):
    sub = lax.broadcasted_iota(jnp.int32, (256, 256), 0)
    lane = lax.broadcasted_iota(jnp.int32, (256, 256), 1)
    for i, (ref, start) in enumerate(((lx_ref, 0), (ly_ref, 0), (sx_ref, 0), (sy_ref, SLAB - 24))):
        n = ref.shape[0]
        taps = jnp.broadcast_to(ref[...].astype(F32)[None, :], (8, n)).astype(BF)
        for row, source in ((i, lane - start), (i + 4, n - 1 - lane + start)):
            spread = jnp.where(sub[:n] == source[:n], 1.0, 0.0).astype(BF)
            out_ref[row : row + 1] = dot(taps, spread)[:1]


def pack_slabs(packed, even_ref, odd_ref):
    right = packed[:, 16:48].reshape(768, 128)
    left = packed[:, :SLAB].reshape(768, 128)
    odd, _ = place("ty")
    even_ref[2304:] = pick(odd, left, right)
    odd_ref[2304:] = pick(odd, right, left)


def pack_x(packed, even_ref, odd_ref):
    right = halves(packed[..., 64:])
    left = halves(packed[..., :64])
    odd, _ = place("tx")
    even_ref[TILE:] = pick(odd, left, right)
    odd_ref[TILE:] = pick(odd, right, left)


def pack_kernel(member_ref, static_ref, first_ref, even_ref, odd_ref, own_ref):
    first_ref[...] = member_ref[0]
    second = member_ref[1].reshape(2304, 128)
    even_ref[:2304] = second
    odd_ref[:2304] = second
    packed = halves(static_ref[...])
    own_ref[...] = packed
    pack_slabs(packed, even_ref, odd_ref)


def first_y_kernel(row_m, row_s, taps_ref, sent_ref, own_ref, even_ref, odd_ref, to_even_ref, to_odd_ref, out_ref):
    member = band_swapped(taps_ref[row_m : row_m + 1], "ty")
    static = band(taps_ref[row_s : row_s + 1], TILE, 112)

    def member_line(x):
        at = pl.ds(pl.multiple_of(x * TILE, TILE), TILE)
        return jnp.concatenate([even_ref[at], sent_ref[at], odd_ref[at]], axis=0)

    def member_store(x, out):
        out = out.astype(BF)
        to_even_ref[x] = out
        to_odd_ref[x] = out

    along_y(member, member_line, TILE, member_store)

    def static_line(x):
        at = pl.ds(pl.multiple_of(2304 + x * SLAB, SLAB), SLAB)
        left, right = sides(even_ref[at], odd_ref[at], "ty")
        return jnp.concatenate([left, own_ref[x], right], axis=0)

    def static_store(x, out):
        out_ref[x] = out.astype(BF)

    along_y(static, static_line, 24, static_store)
    pack_x(out_ref[...], to_even_ref, to_odd_ref)


def first_x_kernel(row, taps_ref, own_ref, even_ref, odd_ref, out_ref):
    matrix = band_swapped(taps_ref[row : row + 1], "tx")
    for c in range(0, TILE, 16):
        at = slice(c, c + 16)
        out_ref[:, at] = along_x(matrix, [even_ref[:, at], own_ref[:, at], odd_ref[:, at]])


def second_y(row, taps_ref, own_ref, even_ref, odd_ref, store):
    matrix = band_swapped(taps_ref[row : row + 1], "ty")

    def line(x):
        return jnp.concatenate([even_ref[x], own_ref[x], odd_ref[x]], axis=0)

    along_y(matrix, line, TILE, store)


def second_x(cols, rows, taps_ref, own_ref, even_ref, odd_ref, s_ref, block):
    matrix = band_swapped(taps_ref[rows[0] : rows[0] + 1], "tx")
    matrix_s = band(taps_ref[rows[1] : rows[1] + 1], 24, 72)
    for c in range(cols[0], cols[1], 16):
        at = slice(c, c + 16)
        b = along_x(matrix, [even_ref[:TILE, at], own_ref[:TILE, at], odd_ref[:TILE, at]])
        left, right = sides(even_ref[TILE:, at], odd_ref[TILE:, at], "tx")
        lines = static_parts(left, s_ref[:, at], right)
        block(at, b, along_x(matrix_s, [lines]))


def static_block(static_ref):
    full = static_ref[...]
    cols = jnp.where(lax.axis_index("mem") == 0, full[:, :64], full[:, 64:])
    zero = jnp.zeros_like(cols)
    return jnp.concatenate([jnp.concatenate([cols, zero], axis=1), jnp.concatenate([zero, cols], axis=1)], axis=0)


def dot_t(a, b):
    return lax.dot_general(a, b, (((1,), (1,)), ((), ())), preferred_element_type=F32)


def forward_a_kernel(row, taps_ref, own_ref, even_ref, odd_ref, pert_ref, vert_ref, out_ref, filtered):
    def store(x, out):
        filtered[x] = out.astype(BF)

    second_y(row, taps_ref, own_ref, even_ref, odd_ref, store)
    vert = vert_ref[...]

    def step(i, carry):
        at = pl.ds(8 * i, 8)
        local = dot_t(filtered[at].reshape(384, 128), vert).reshape(8, TILE, 128)
        out_ref[at] = pert_ref[0, at].astype(F32) * local
        return carry

    lax.fori_loop(0, 6, step, 0, unroll=6)


def forward_b_kernel(
    cols, rows, taps_ref, own_ref, even_ref, odd_ref, s_ref, first_ref, pert_ref, vert_ref, static_ref,
    after_ref, kept_ref, sent_ref
):
    vert = vert_ref[...]
    static_mat = static_block(static_ref)

    def block(at, b, s):
        total = first_ref[:, at]
        total += pert_ref[1, :, at].astype(F32) * dot_t(b.reshape(768, 128), vert).reshape(TILE, 16, 128)
        static = dot_t(s.reshape(384, 128), static_mat)
        total += jnp.concatenate([static[:, :128], static[:, 128:]], axis=0).reshape(TILE, 16, 128)
        to = slice(at.start - cols[0], at.stop - cols[0])
        kept_ref[:, to] = total
        sent_ref[:, to] = total.astype(BF)

    second_x(cols, rows, taps_ref, own_ref, even_ref, odd_ref, s_ref, block)


def residual_kernel(
    kept0, came0, kept1, came1, dep_ref, weight_ref, pert_ref, vert_ref, static_ref, even_ref, odd_ref, own_ref, b_ref
):
    vert = vert_ref[...]
    static_mat = static_block(static_ref)

    def step(i, carry):
        res = []
        for x in (4 * i, 24 + 4 * i):
            at = pl.ds(x, 4)
            parts = [kept[at] + came[at].astype(F32) for kept, came in ((kept0, came0), (kept1, came1))]
            total = jnp.concatenate(parts, axis=1)
            r = (weight_ref[at].astype(F32) * (total - dep_ref[at].astype(F32))).astype(BF)
            r32 = r.astype(F32)
            res.append(r.reshape(192, 128))
            first = (pert_ref[0, at].astype(F32) * r32).astype(BF).reshape(192, 128)
            second = (pert_ref[1, at].astype(F32) * r32).astype(BF).reshape(192, 128)
            back = dot(first, vert).astype(BF).reshape(4, TILE, 128)
            even_ref[at] = back
            odd_ref[at] = back
            b_ref[at] = dot(second, vert).astype(BF).reshape(4, TILE, 128)
        static = dot(jnp.concatenate(res, axis=1), static_mat).astype(BF)
        own_ref[pl.ds(4 * i, 4)] = static.reshape(4, TILE, 128)
        return carry

    lax.fori_loop(0, 6, step, 0, unroll=6)
    pack_x(own_ref[...], even_ref, odd_ref)


def back_x_kernel(
    rows, taps_ref, sent_ref, own_ref, even_ref, odd_ref, after_ref, to_even_ref, to_odd_ref, slab_ref, out_ref
):
    member = band_swapped(taps_ref[rows[0] : rows[0] + 1], "tx")
    static = band(taps_ref[rows[1] : rows[1] + 1], 24, 72)
    for c in range(0, TILE, 16):
        at = slice(c, c + 16)
        out = along_x(member, [even_ref[:TILE, at], sent_ref[:TILE, at], odd_ref[:TILE, at]])
        to_even_ref[:TILE, at] = out
        to_odd_ref[:, at] = out
        left, right = sides(even_ref[TILE:, at], odd_ref[TILE:, at], "tx")
        out_ref[:, at] = along_x(static, [static_parts(left, own_ref[:, at], right)])
    packed = out_ref[...]
    right = packed[:, 16:48].reshape(16, TILE, 128)
    left = packed[:, :SLAB].reshape(16, TILE, 128)
    odd, _ = place("ty")
    to_even_ref[TILE:] = pick(odd, left, right)
    slab_ref[...] = pick(odd, right, left)


def back_y_kernel(row, taps_ref, own_ref, even_ref, odd_ref, out_ref):
    def store(x, out):
        out_ref[x] = out.astype(BF)

    second_y(row, taps_ref, own_ref, even_ref, odd_ref, store)


def last_b_kernel(row, taps_ref, own_ref, even_ref, odd_ref, member_ref, member_out, member, sems):
    matrix = band_swapped(taps_ref[row : row + 1], "tx")
    copies = []
    for i in range(3):
        at = slice(16 * i, 16 * i + 16)
        b = along_x(matrix, [even_ref[:, at], own_ref[:, at], odd_ref[:, at]])
        member[i] = (member_ref[1, :, at].astype(F32) + b.astype(F32)).astype(BF)
        copies.append(pltpu.make_async_copy(member.at[i], member_out.at[1, :, at], sems.at[i]))
        copies[i].start()
    for copy in copies:
        copy.wait()


def last_a_kernel(
    rows, taps_ref, own_ref, even_ref, odd_ref, slab_ref, s_ref, member_ref, control_ref, begun_ref,
    static_out, member_out, static, member, sems
):
    copies = []

    def send(source, target):
        copies.append(pltpu.make_async_copy(source, target, sems.at[len(copies)]))
        copies[-1].start()

    matrix = band(taps_ref[rows[1] : rows[1] + 1], TILE, 112)
    slabs = [r.reshape(24, SLAB, 128) for r in (even_ref[TILE:], slab_ref[...])]
    left, right = sides(slabs[0], slabs[1], "ty")
    for x in range(0, 24, 2):
        lines = [jnp.concatenate([left[k], s_ref[k], right[k]], axis=0) for k in (x, x + 1)]
        out = dot(matrix, jnp.concatenate(lines, axis=1)).astype(BF).astype(F32)
        for k in (0, 1):
            both = (control_ref[x + k].astype(F32) + out[:, 128 * k : 128 * k + 128]).astype(BF)
            static[x + k] = both[:, :64]
            static[x + k + 24] = both[:, 64:]
        if x % 12 == 10:
            for part in (pl.ds(x - 10, 12), pl.ds(x + 14, 12)):
                send(static.at[part], static_out.at[part])
    matrix = band_swapped(taps_ref[rows[0] : rows[0] + 1], "ty")
    for first in range(0, TILE, 12):

        def line(x):
            x = first + x
            return jnp.concatenate([even_ref[x], own_ref[x], odd_ref[x]], axis=0)

        def store(x, out):
            x = first + x
            member[x] = (member_ref[0, x].astype(F32) + out.astype(BF).astype(F32)).astype(BF)

        along_y(matrix, line, 12, store)
        part = pl.ds(first, 12)
        send(member.at[part], member_out.at[0, part])
    for copy in copies:
        copy.wait()


def swaps_y(even, *odd):
    n = lax.axis_size("ty")
    first = [(i, i ^ 1) for i in range(n)]
    second = [(i, (i + 1) % n if i % 2 else (i - 1) % n) for i in range(n)]
    return (lax.ppermute(even, "ty", first),) + tuple(lax.ppermute(part, "ty", second) for part in odd)


def swaps_x(even, odd):
    n, m = lax.axis_size("tx"), lax.axis_size("ty")
    first = [(i, i ^ 1) for i in range(n)]
    second = []
    for i in range(n):
        other = i + 1 if i % 2 else i - 1
        for j in range(m):
            second.append((i * m + j, i * m + (j ^ 1) if i in (0, n - 1) else other * m + j))
    return lax.ppermute(even, "tx", first), lax.ppermute(odd, ("tx", "ty"), second)


def first_filters(taps, a, to_even, to_odd, own):
    a_halo = swaps_x(a, a)
    b_halo = swaps_y(to_even, to_odd)
    tile = (TILE, TILE, 128)
    b_to_even, b_to_odd, s = call(
        functools.partial(first_y_kernel, 1, 3),
        (shape(60, TILE, 128), shape(60, TILE, 128), shape(24, TILE, 128)),
        (taps, to_even, own) + b_halo,
        700_000_000,
    )
    b_halo = swaps_x(b_to_even, b_to_odd)
    (a,) = call(functools.partial(first_x_kernel, 0), (shape(*tile),), (taps, a) + a_halo, 500_000_000)
    a_halo = swaps_y(a, a)
    return (a,) + a_halo, (b_to_even,) + b_halo + (s,)


def body(
    static_control,
    member_control,
    perturbations,
    departures,
    obs_weight,
    static_kx,
    static_ky,
    local_kx,
    local_ky,
    static_vertical,
    local_vertical,
):
    (taps,) = call(
        taps_kernel, (shape(8, 256, dtype=F32),), (local_kx, local_ky, static_kx, static_ky), BRIEF
    )
    tile = (TILE, TILE, 128)
    sent_shapes = (shape(3072, 128), shape(3072, 128), shape(24, TILE, 128))

    a, to_even, to_odd, control = call(
        pack_kernel, (shape(*tile),) + sent_shapes, (member_control, static_control), 1_000_000
    )
    a, b = first_filters(taps, a, to_even, to_odd, control)
    (first,) = call(
        functools.partial(forward_a_kernel, 1), (shape(*tile, dtype=F32),),
        (taps,) + a + (perturbations, local_vertical), 800_000_000, [pltpu.VMEM(tile, BF)],
    )
    size = lax.axis_size("mem")
    parts, sent = (), first
    for cols, cost in (((0, 32), 700_000_000), ((32, TILE), LONG)):
        wide = (TILE, cols[1] - cols[0], 128)
        args = (taps,) + b + (first, perturbations, local_vertical, static_vertical, sent)
        kept, sent = call(
            functools.partial(forward_b_kernel, cols, (0, 2)), (shape(*wide, dtype=F32), shape(*wide)),
            args, cost, in_any=(len(args) - 1,),
        )
        parts += (kept, lax.ppermute(sent, "mem", [(i, size - 1 - i) for i in range(size)]))

    to_even, to_odd, own, b = call(
        residual_kernel, (shape(60, TILE, 128), shape(60, TILE, 128), shape(24, TILE, 128), shape(*tile)),
        parts + (departures, obs_weight, perturbations, local_vertical, static_vertical), 400_000_000,
    )
    a = (to_even, own) + swaps_x(to_even, to_odd)
    (b,) = call(functools.partial(back_y_kernel, 5), (shape(*tile),), (taps, b) + swaps_y(b, b), BRIEF)
    b_halo = swaps_x(b, b)
    args = (taps,) + a + (b,)
    to_even, to_odd, slab, s = call(
        functools.partial(back_x_kernel, (4, 6)),
        (shape(64, TILE, 128), shape(*tile), shape(16, TILE, 128), shape(24, TILE, 128)), args, LONG,
        in_any=(len(args) - 1,),
    )
    a = (to_even,) + swaps_y(to_even, to_odd, slab) + (s,)
    (begun,) = call(
        functools.partial(last_b_kernel, 4), (shape(2, *tile),), (taps, b) + b_halo + (member_control,), LONG,
        [pltpu.VMEM((3, TILE, 16, 128), BF), pltpu.SemaphoreType.DMA((3,))], out_any=(0,),
    )
    args = (taps,) + a + (member_control, control, begun)
    return tuple(call(
        functools.partial(last_a_kernel, (5, 7)), (shape(TILE, TILE, 64), shape(2, *tile)), args, 700_000_000,
        [pltpu.VMEM((TILE, TILE, 64), BF), pltpu.VMEM(tile, BF), pltpu.SemaphoreType.DMA((8,))],
        in_any=(len(args) - 1,), out_any=(0, 1), aliases={len(args) - 1: 1},
    ))


def solution(mesh):
    return jax.shard_map(
        body,
        mesh=mesh,
        in_specs=(
            P("tx", "ty", "mem"),
            P("mem", "tx", "ty", None),
            P("mem", "tx", "ty", None),
            P("tx", "ty", None),
            P("tx", "ty", None),
            P(),
            P(),
            P(),
            P(),
            P(),
            P(),
        ),
        out_specs=(P("tx", "ty", "mem"), P("mem", "tx", "ty", None)),
        check_vma=False,
    )
```

```python
import functools

import jax
import jax.numpy as jnp
from jax import lax
from jax.experimental import pallas as pl
from jax.experimental.pallas import tpu as pltpu
from jax.sharding import PartitionSpec as P

TILE = 48
SLAB = 32
BRIEF = 1_000
LONG = 20_000_000_000
BF = jnp.bfloat16
F32 = jnp.float32


VMEM = pl.BlockSpec(memory_space=pltpu.VMEM)
ANY = pl.BlockSpec(memory_space=pl.ANY)


def call(kernel, out_shape, args, flops, scratch=(), in_any=(), out_any=(), aliases=None):
    outs = tuple(out_shape)
    moved = sum(a.size * a.dtype.itemsize for a in args)
    moved += sum(o.size * jnp.dtype(o.dtype).itemsize for o in outs)
    return pl.pallas_call(
        kernel,
        out_shape=outs,
        in_specs=[ANY if i in in_any else VMEM for i in range(len(args))],
        out_specs=tuple(ANY if i in out_any else VMEM for i in range(len(outs))),
        scratch_shapes=list(scratch),
        input_output_aliases=aliases or {},
        compiler_params=pltpu.CompilerParams(vmem_limit_bytes=20 << 20),
        cost_estimate=pl.CostEstimate(flops=flops, bytes_accessed=min(moved, flops), transcendentals=0),
    )(*args)


def shape(*sizes, dtype=BF):
    return jax.ShapeDtypeStruct(sizes, dtype)


def band(row, rows, cols):
    spread = jnp.broadcast_to(row, (rows, row.shape[1]))
    return pltpu.roll(spread, 0, 1, stride=1, stride_axis=0)[:, :cols].astype(BF)


def place(axis):
    at = lax.axis_index(axis)
    return at % 2 == 1, (at == 0) | (at == lax.axis_size(axis) - 1)


def band_swapped(row, axis):
    spread = jnp.broadcast_to(row, (TILE, row.shape[1]))
    plain = pltpu.roll(spread, 0, 1, stride=1, stride_axis=0)
    right = pltpu.roll(spread, row.shape[1] - 96, 1, stride=1, stride_axis=0)
    left = pltpu.roll(spread, 96, 1, stride=1, stride_axis=0)
    lane = lax.broadcasted_iota(jnp.int32, plain.shape, 1)
    odd, end = place(axis)
    turned = jnp.where(lane < 48, right, jnp.where(lane < 96, plain, left))
    both = jnp.where(jnp.full(plain.shape, odd.astype(jnp.int32)) == 1, plain, turned)
    keep = (lane < 96) | (jnp.full(plain.shape, end.astype(jnp.int32)) == 0)
    return jnp.where(keep, both, 0.0)[:, :144].astype(BF)


def pick(odd, a, b):
    return jnp.where(odd, a, b)


def sides(even, odd_swap, axis):
    odd, end = place(axis)
    outer = pick(end, jnp.zeros_like(odd_swap), odd_swap)
    return pick(odd, even, outer), pick(odd, outer, even)


def halves(a):
    return jnp.concatenate([a[: a.shape[0] // 2], a[a.shape[0] // 2 :]], axis=-1)


def unhalves(a):
    n = a.shape[-1] // 2
    return jnp.concatenate([a[..., :n], a[..., n:]], axis=0)


def dot(a, b):
    return jnp.dot(a, b, preferred_element_type=F32)


def along_y(matrix, line, count, store):
    def step(i, carry):
        pair = jnp.concatenate([line(2 * i), line(2 * i + 1)], axis=1)
        out = dot(matrix, pair)
        store(2 * i, out[:, :128])
        store(2 * i + 1, out[:, 128:])
        return carry

    lax.fori_loop(0, count // 2, step, 0, unroll=count // 2)


def along_x(matrix, parts):
    turned = [jnp.swapaxes(p, 0, 1) for p in parts]
    outs = []
    for j in range(0, 16, 2):
        cols = [
            jnp.concatenate([t[j + k] for t in turned], axis=0) if len(turned) > 1 else turned[0][j + k]
            for k in (0, 1)
        ]
        out = dot(matrix, jnp.concatenate(cols, axis=1))
        outs += [out[:, :128].astype(BF), out[:, 128:].astype(BF)]
    return jnp.swapaxes(jnp.stack(outs), 0, 1)


def static_parts(left, own, right):
    swap = jnp.concatenate([own[..., 64:], own[..., :64]], axis=-1)
    first = jnp.concatenate([unhalves(left), swap[..., 64:]], axis=-1)
    last = jnp.concatenate([swap[..., :64], unhalves(right)], axis=-1)
    return jnp.concatenate([first, own, last], axis=0)


def taps_kernel(lx_ref, ly_ref, sx_ref, sy_ref, out_ref):
    sub = lax.broadcasted_iota(jnp.int32, (256, 256), 0)
    lane = lax.broadcasted_iota(jnp.int32, (256, 256), 1)
    for i, (ref, start) in enumerate(((lx_ref, 0), (ly_ref, 0), (sx_ref, 0), (sy_ref, SLAB - 24))):
        n = ref.shape[0]
        taps = jnp.broadcast_to(ref[...].astype(F32)[None, :], (8, n)).astype(BF)
        for row, source in ((i, lane - start), (i + 4, n - 1 - lane + start)):
            spread = jnp.where(sub[:n] == source[:n], 1.0, 0.0).astype(BF)
            out_ref[row : row + 1] = dot(taps, spread)[:1]


def pack_slabs(packed, even_ref, odd_ref):
    right = packed[:, 16:48].reshape(768, 128)
    left = packed[:, :SLAB].reshape(768, 128)
    odd, _ = place("ty")
    even_ref[2304:] = pick(odd, left, right)
    odd_ref[2304:] = pick(odd, right, left)


def pack_x(packed, even_ref, odd_ref):
    right = halves(packed[..., 64:])
    left = halves(packed[..., :64])
    odd, _ = place("tx")
    even_ref[TILE:] = pick(odd, left, right)
    odd_ref[TILE:] = pick(odd, right, left)


def pack_kernel(member_ref, static_ref, first_ref, even_ref, odd_ref, own_ref):
    first_ref[...] = member_ref[0]
    second = member_ref[1].reshape(2304, 128)
    even_ref[:2304] = second
    odd_ref[:2304] = second
    packed = halves(static_ref[...])
    own_ref[...] = packed
    pack_slabs(packed, even_ref, odd_ref)


def first_y_kernel(row_m, row_s, taps_ref, sent_ref, own_ref, even_ref, odd_ref, to_even_ref, to_odd_ref, out_ref):
    member = band_swapped(taps_ref[row_m : row_m + 1], "ty")
    static = band(taps_ref[row_s : row_s + 1], TILE, 112)

    def member_line(x):
        at = pl.ds(pl.multiple_of(x * TILE, TILE), TILE)
        return jnp.concatenate([even_ref[at], sent_ref[at], odd_ref[at]], axis=0)

    def member_store(x, out):
        out = out.astype(BF)
        to_even_ref[x] = out
        to_odd_ref[x] = out

    along_y(member, member_line, TILE, member_store)

    def static_line(x):
        at = pl.ds(pl.multiple_of(2304 + x * SLAB, SLAB), SLAB)
        left, right = sides(even_ref[at], odd_ref[at], "ty")
        return jnp.concatenate([left, own_ref[x], right], axis=0)

    def static_store(x, out):
        out_ref[x] = out.astype(BF)

    along_y(static, static_line, 24, static_store)
    pack_x(out_ref[...], to_even_ref, to_odd_ref)


def first_x_kernel(row, taps_ref, own_ref, even_ref, odd_ref, out_ref):
    matrix = band_swapped(taps_ref[row : row + 1], "tx")
    for c in range(0, TILE, 16):
        at = slice(c, c + 16)
        out_ref[:, at] = along_x(matrix, [even_ref[:, at], own_ref[:, at], odd_ref[:, at]])


def second_y(row, taps_ref, own_ref, even_ref, odd_ref, store):
    matrix = band_swapped(taps_ref[row : row + 1], "ty")

    def line(x):
        return jnp.concatenate([even_ref[x], own_ref[x], odd_ref[x]], axis=0)

    along_y(matrix, line, TILE, store)


def second_x(cols, rows, taps_ref, own_ref, even_ref, odd_ref, s_ref, block):
    matrix = band_swapped(taps_ref[rows[0] : rows[0] + 1], "tx")
    matrix_s = band(taps_ref[rows[1] : rows[1] + 1], 24, 72)
    for c in range(cols[0], cols[1], 16):
        at = slice(c, c + 16)
        b = along_x(matrix, [even_ref[:TILE, at], own_ref[:TILE, at], odd_ref[:TILE, at]])
        left, right = sides(even_ref[TILE:, at], odd_ref[TILE:, at], "tx")
        lines = static_parts(left, s_ref[:, at], right)
        block(at, b, along_x(matrix_s, [lines]))


def static_block(static_ref):
    full = static_ref[...]
    cols = jnp.where(lax.axis_index("mem") == 0, full[:, :64], full[:, 64:])
    zero = jnp.zeros_like(cols)
    return jnp.concatenate([jnp.concatenate([cols, zero], axis=1), jnp.concatenate([zero, cols], axis=1)], axis=0)


def dot_t(a, b):
    return lax.dot_general(a, b, (((1,), (1,)), ((), ())), preferred_element_type=F32)


def forward_a_kernel(row, taps_ref, own_ref, even_ref, odd_ref, pert_ref, vert_ref, out_ref, filtered):
    def store(x, out):
        filtered[x] = out.astype(BF)

    second_y(row, taps_ref, own_ref, even_ref, odd_ref, store)
    vert = vert_ref[...]

    def step(i, carry):
        at = pl.ds(8 * i, 8)
        local = dot_t(filtered[at].reshape(384, 128), vert).reshape(8, TILE, 128)
        out_ref[at] = pert_ref[0, at].astype(F32) * local
        return carry

    lax.fori_loop(0, 6, step, 0, unroll=6)


def forward_b_kernel(
    cols, rows, taps_ref, own_ref, even_ref, odd_ref, s_ref, first_ref, pert_ref, vert_ref, static_ref,
    after_ref, kept_ref, sent_ref
):
    vert = vert_ref[...]
    static_mat = static_block(static_ref)

    def block(at, b, s):
        total = first_ref[:, at]
        total += pert_ref[1, :, at].astype(F32) * dot_t(b.reshape(768, 128), vert).reshape(TILE, 16, 128)
        static = dot_t(s.reshape(384, 128), static_mat)
        total += jnp.concatenate([static[:, :128], static[:, 128:]], axis=0).reshape(TILE, 16, 128)
        to = slice(at.start - cols[0], at.stop - cols[0])
        kept_ref[:, to] = total
        sent_ref[:, to] = total.astype(BF)

    second_x(cols, rows, taps_ref, own_ref, even_ref, odd_ref, s_ref, block)


def residual_kernel(
    kept0, came0, kept1, came1, kept2, came2, dep_ref, weight_ref, pert_ref, vert_ref, static_ref, even_ref, odd_ref, own_ref, b_ref
):
    vert = vert_ref[...]
    static_mat = static_block(static_ref)

    def step(i, carry):
        res = []
        for x in (4 * i, 24 + 4 * i):
            at = pl.ds(x, 4)
            pairs = ((kept0, came0), (kept1, came1), (kept2, came2))
            parts = [kept[at] + came[at].astype(F32) for kept, came in pairs]
            total = jnp.concatenate(parts, axis=1)
            r = (weight_ref[at].astype(F32) * (total - dep_ref[at].astype(F32))).astype(BF)
            r32 = r.astype(F32)
            res.append(r.reshape(192, 128))
            first = (pert_ref[0, at].astype(F32) * r32).astype(BF).reshape(192, 128)
            second = (pert_ref[1, at].astype(F32) * r32).astype(BF).reshape(192, 128)
            back = dot(first, vert).astype(BF).reshape(4, TILE, 128)
            even_ref[at] = back
            odd_ref[at] = back
            b_ref[at] = dot(second, vert).astype(BF).reshape(4, TILE, 128)
        static = dot(jnp.concatenate(res, axis=1), static_mat).astype(BF)
        own_ref[pl.ds(4 * i, 4)] = static.reshape(4, TILE, 128)
        return carry

    lax.fori_loop(0, 6, step, 0, unroll=6)
    pack_x(own_ref[...], even_ref, odd_ref)


def back_x_kernel(
    rows, taps_ref, sent_ref, own_ref, even_ref, odd_ref, after_ref, to_even_ref, to_odd_ref, slab_ref, out_ref
):
    member = band_swapped(taps_ref[rows[0] : rows[0] + 1], "tx")
    static = band(taps_ref[rows[1] : rows[1] + 1], 24, 72)
    for c in range(0, TILE, 16):
        at = slice(c, c + 16)
        out = along_x(member, [even_ref[:TILE, at], sent_ref[:TILE, at], odd_ref[:TILE, at]])
        to_even_ref[:TILE, at] = out
        to_odd_ref[:, at] = out
        left, right = sides(even_ref[TILE:, at], odd_ref[TILE:, at], "tx")
        out_ref[:, at] = along_x(static, [static_parts(left, own_ref[:, at], right)])
    packed = out_ref[...]
    right = packed[:, 16:48].reshape(16, TILE, 128)
    left = packed[:, :SLAB].reshape(16, TILE, 128)
    odd, _ = place("ty")
    to_even_ref[TILE:] = pick(odd, left, right)
    slab_ref[...] = pick(odd, right, left)


def back_y_kernel(row, taps_ref, own_ref, even_ref, odd_ref, out_ref):
    def store(x, out):
        out_ref[x] = out.astype(BF)

    second_y(row, taps_ref, own_ref, even_ref, odd_ref, store)


def last_b_kernel(row, taps_ref, own_ref, even_ref, odd_ref, member_ref, member_out, member, sems):
    matrix = band_swapped(taps_ref[row : row + 1], "tx")
    copies = []
    for i in range(3):
        at = slice(16 * i, 16 * i + 16)
        b = along_x(matrix, [even_ref[:, at], own_ref[:, at], odd_ref[:, at]])
        member[i] = (member_ref[1, :, at].astype(F32) + b.astype(F32)).astype(BF)
        copies.append(pltpu.make_async_copy(member.at[i], member_out.at[1, :, at], sems.at[i]))
        copies[i].start()
    for copy in copies:
        copy.wait()


def last_a_kernel(
    rows, taps_ref, own_ref, even_ref, odd_ref, slab_ref, s_ref, member_ref, control_ref, begun_ref,
    static_out, member_out, static, member, sems
):
    copies = []

    def send(source, target):
        copies.append(pltpu.make_async_copy(source, target, sems.at[len(copies)]))
        copies[-1].start()

    matrix = band(taps_ref[rows[1] : rows[1] + 1], TILE, 112)
    slabs = [r.reshape(24, SLAB, 128) for r in (even_ref[TILE:], slab_ref[...])]
    left, right = sides(slabs[0], slabs[1], "ty")
    for x in range(0, 24, 2):
        lines = [jnp.concatenate([left[k], s_ref[k], right[k]], axis=0) for k in (x, x + 1)]
        out = dot(matrix, jnp.concatenate(lines, axis=1)).astype(BF).astype(F32)
        for k in (0, 1):
            both = (control_ref[x + k].astype(F32) + out[:, 128 * k : 128 * k + 128]).astype(BF)
            static[x + k] = both[:, :64]
            static[x + k + 24] = both[:, 64:]
        if x % 12 == 10:
            for part in (pl.ds(x - 10, 12), pl.ds(x + 14, 12)):
                send(static.at[part], static_out.at[part])
    matrix = band_swapped(taps_ref[rows[0] : rows[0] + 1], "ty")
    for first in range(0, TILE, 12):

        def line(x):
            x = first + x
            return jnp.concatenate([even_ref[x], own_ref[x], odd_ref[x]], axis=0)

        def store(x, out):
            x = first + x
            member[x] = (member_ref[0, x].astype(F32) + out.astype(BF).astype(F32)).astype(BF)

        along_y(matrix, line, 12, store)
        part = pl.ds(first, 12)
        send(member.at[part], member_out.at[0, part])
    for copy in copies:
        copy.wait()


def swaps_y(even, *odd):
    n = lax.axis_size("ty")
    first = [(i, i ^ 1) for i in range(n)]
    second = [(i, (i + 1) % n if i % 2 else (i - 1) % n) for i in range(n)]
    return (lax.ppermute(even, "ty", first),) + tuple(lax.ppermute(part, "ty", second) for part in odd)


def swaps_x(even, odd):
    n, m = lax.axis_size("tx"), lax.axis_size("ty")
    first = [(i, i ^ 1) for i in range(n)]
    second = []
    for i in range(n):
        other = i + 1 if i % 2 else i - 1
        for j in range(m):
            second.append((i * m + j, i * m + (j ^ 1) if i in (0, n - 1) else other * m + j))
    return lax.ppermute(even, "tx", first), lax.ppermute(odd, ("tx", "ty"), second)


def first_filters(taps, a, to_even, to_odd, own):
    a_halo = swaps_x(a, a)
    b_halo = swaps_y(to_even, to_odd)
    tile = (TILE, TILE, 128)
    b_to_even, b_to_odd, s = call(
        functools.partial(first_y_kernel, 1, 3),
        (shape(60, TILE, 128), shape(60, TILE, 128), shape(24, TILE, 128)),
        (taps, to_even, own) + b_halo,
        700_000_000,
    )
    b_halo = swaps_x(b_to_even, b_to_odd)
    (a,) = call(functools.partial(first_x_kernel, 0), (shape(*tile),), (taps, a) + a_halo, 500_000_000)
    a_halo = swaps_y(a, a)
    return (a,) + a_halo, (b_to_even,) + b_halo + (s,)


def body(
    static_control,
    member_control,
    perturbations,
    departures,
    obs_weight,
    static_kx,
    static_ky,
    local_kx,
    local_ky,
    static_vertical,
    local_vertical,
):
    (taps,) = call(
        taps_kernel, (shape(8, 256, dtype=F32),), (local_kx, local_ky, static_kx, static_ky), BRIEF
    )
    tile = (TILE, TILE, 128)
    sent_shapes = (shape(3072, 128), shape(3072, 128), shape(24, TILE, 128))

    a, to_even, to_odd, control = call(
        pack_kernel, (shape(*tile),) + sent_shapes, (member_control, static_control), 1_000_000
    )
    a, b = first_filters(taps, a, to_even, to_odd, control)
    (first,) = call(
        functools.partial(forward_a_kernel, 1), (shape(*tile, dtype=F32),),
        (taps,) + a + (perturbations, local_vertical), 800_000_000, [pltpu.VMEM(tile, BF)],
    )
    size = lax.axis_size("mem")
    parts, sent = (), first
    for cols, cost in (((0, 16), 700_000_000), ((16, 32), LONG), ((32, TILE), LONG)):
        wide = (TILE, cols[1] - cols[0], 128)
        args = (taps,) + b + (first, perturbations, local_vertical, static_vertical, sent)
        kept, sent = call(
            functools.partial(forward_b_kernel, cols, (0, 2)), (shape(*wide, dtype=F32), shape(*wide)),
            args, cost, in_any=(len(args) - 1,),
        )
        parts += (kept, lax.ppermute(sent, "mem", [(i, size - 1 - i) for i in range(size)]))

    to_even, to_odd, own, b = call(
        residual_kernel, (shape(60, TILE, 128), shape(60, TILE, 128), shape(24, TILE, 128), shape(*tile)),
        parts + (departures, obs_weight, perturbations, local_vertical, static_vertical), 400_000_000,
    )
    a = (to_even, own) + swaps_x(to_even, to_odd)
    (b,) = call(functools.partial(back_y_kernel, 5), (shape(*tile),), (taps, b) + swaps_y(b, b), BRIEF)
    b_halo = swaps_x(b, b)
    args = (taps,) + a + (b,)
    to_even, to_odd, slab, s = call(
        functools.partial(back_x_kernel, (4, 6)),
        (shape(64, TILE, 128), shape(*tile), shape(16, TILE, 128), shape(24, TILE, 128)), args, LONG,
        in_any=(len(args) - 1,),
    )
    a = (to_even,) + swaps_y(to_even, to_odd, slab) + (s,)
    (begun,) = call(
        functools.partial(last_b_kernel, 4), (shape(2, *tile),), (taps, b) + b_halo + (member_control,), LONG,
        [pltpu.VMEM((3, TILE, 16, 128), BF), pltpu.SemaphoreType.DMA((3,))], out_any=(0,),
    )
    args = (taps,) + a + (member_control, control, begun)
    return tuple(call(
        functools.partial(last_a_kernel, (5, 7)), (shape(TILE, TILE, 64), shape(2, *tile)), args, 700_000_000,
        [pltpu.VMEM((TILE, TILE, 64), BF), pltpu.VMEM(tile, BF), pltpu.SemaphoreType.DMA((8,))],
        in_any=(len(args) - 1,), out_any=(0, 1), aliases={len(args) - 1: 1},
    ))


def solution(mesh):
    return jax.shard_map(
        body,
        mesh=mesh,
        in_specs=(
            P("tx", "ty", "mem"),
            P("mem", "tx", "ty", None),
            P("mem", "tx", "ty", None),
            P("tx", "ty", None),
            P("tx", "ty", None),
            P(),
            P(),
            P(),
            P(),
            P(),
            P(),
        ),
        out_specs=(P("tx", "ty", "mem"), P("mem", "tx", "ty", None)),
        check_vma=False,
    )
```

```python
import functools

import jax
import jax.numpy as jnp
from jax import lax
from jax.experimental import pallas as pl
from jax.experimental.pallas import tpu as pltpu
from jax.sharding import PartitionSpec as P

TILE = 48
SLAB = 32
BRIEF = 1_000
LONG = 20_000_000_000
BF = jnp.bfloat16
F32 = jnp.float32


VMEM = pl.BlockSpec(memory_space=pltpu.VMEM)
ANY = pl.BlockSpec(memory_space=pl.ANY)


def call(kernel, out_shape, args, flops, scratch=(), in_any=(), out_any=(), aliases=None):
    outs = tuple(out_shape)
    moved = sum(a.size * a.dtype.itemsize for a in args)
    moved += sum(o.size * jnp.dtype(o.dtype).itemsize for o in outs)
    return pl.pallas_call(
        kernel,
        out_shape=outs,
        in_specs=[ANY if i in in_any else VMEM for i in range(len(args))],
        out_specs=tuple(ANY if i in out_any else VMEM for i in range(len(outs))),
        scratch_shapes=list(scratch),
        input_output_aliases=aliases or {},
        compiler_params=pltpu.CompilerParams(vmem_limit_bytes=20 << 20),
        cost_estimate=pl.CostEstimate(flops=flops, bytes_accessed=min(moved, flops), transcendentals=0),
    )(*args)


def shape(*sizes, dtype=BF):
    return jax.ShapeDtypeStruct(sizes, dtype)


def band(row, rows, cols):
    spread = jnp.broadcast_to(row, (rows, row.shape[1]))
    return pltpu.roll(spread, 0, 1, stride=1, stride_axis=0)[:, :cols].astype(BF)


def place(axis):
    at = lax.axis_index(axis)
    return at % 2 == 1, (at == 0) | (at == lax.axis_size(axis) - 1)


def band_swapped(row, axis):
    spread = jnp.broadcast_to(row, (TILE, row.shape[1]))
    plain = pltpu.roll(spread, 0, 1, stride=1, stride_axis=0)
    right = pltpu.roll(spread, row.shape[1] - 96, 1, stride=1, stride_axis=0)
    left = pltpu.roll(spread, 96, 1, stride=1, stride_axis=0)
    lane = lax.broadcasted_iota(jnp.int32, plain.shape, 1)
    odd, end = place(axis)
    turned = jnp.where(lane < 48, right, jnp.where(lane < 96, plain, left))
    both = jnp.where(jnp.full(plain.shape, odd.astype(jnp.int32)) == 1, plain, turned)
    keep = (lane < 96) | (jnp.full(plain.shape, end.astype(jnp.int32)) == 0)
    return jnp.where(keep, both, 0.0)[:, :144].astype(BF)


def pick(odd, a, b):
    return jnp.where(odd, a, b)


def sides(even, odd_swap, axis):
    odd, end = place(axis)
    outer = pick(end, jnp.zeros_like(odd_swap), odd_swap)
    return pick(odd, even, outer), pick(odd, outer, even)


def halves(a):
    return jnp.concatenate([a[: a.shape[0] // 2], a[a.shape[0] // 2 :]], axis=-1)


def unhalves(a):
    n = a.shape[-1] // 2
    return jnp.concatenate([a[..., :n], a[..., n:]], axis=0)


def dot(a, b):
    return jnp.dot(a, b, preferred_element_type=F32)


def along_y(matrix, line, count, store):
    def step(i, carry):
        pair = jnp.concatenate([line(2 * i), line(2 * i + 1)], axis=1)
        out = dot(matrix, pair)
        store(2 * i, out[:, :128])
        store(2 * i + 1, out[:, 128:])
        return carry

    lax.fori_loop(0, count // 2, step, 0, unroll=count // 2)


def along_x(matrix, parts):
    turned = [jnp.swapaxes(p, 0, 1) for p in parts]
    outs = []
    for j in range(0, 16, 2):
        cols = [
            jnp.concatenate([t[j + k] for t in turned], axis=0) if len(turned) > 1 else turned[0][j + k]
            for k in (0, 1)
        ]
        out = dot(matrix, jnp.concatenate(cols, axis=1))
        outs += [out[:, :128].astype(BF), out[:, 128:].astype(BF)]
    return jnp.swapaxes(jnp.stack(outs), 0, 1)


def static_parts(left, own, right):
    swap = jnp.concatenate([own[..., 64:], own[..., :64]], axis=-1)
    first = jnp.concatenate([unhalves(left), swap[..., 64:]], axis=-1)
    last = jnp.concatenate([swap[..., :64], unhalves(right)], axis=-1)
    return jnp.concatenate([first, own, last], axis=0)


def taps_kernel(lx_ref, ly_ref, sx_ref, sy_ref, out_ref):
    sub = lax.broadcasted_iota(jnp.int32, (256, 256), 0)
    lane = lax.broadcasted_iota(jnp.int32, (256, 256), 1)
    for i, (ref, start) in enumerate(((lx_ref, 0), (ly_ref, 0), (sx_ref, 0), (sy_ref, SLAB - 24))):
        n = ref.shape[0]
        taps = jnp.broadcast_to(ref[...].astype(F32)[None, :], (8, n)).astype(BF)
        for row, source in ((i, lane - start), (i + 4, n - 1 - lane + start)):
            spread = jnp.where(sub[:n] == source[:n], 1.0, 0.0).astype(BF)
            out_ref[row : row + 1] = dot(taps, spread)[:1]


def pack_slabs(packed, even_ref, odd_ref):
    right = packed[:, 16:48].reshape(768, 128)
    left = packed[:, :SLAB].reshape(768, 128)
    odd, _ = place("ty")
    even_ref[2304:] = pick(odd, left, right)
    odd_ref[2304:] = pick(odd, right, left)


def pack_x(packed, even_ref, odd_ref):
    right = halves(packed[..., 64:])
    left = halves(packed[..., :64])
    odd, _ = place("tx")
    even_ref[TILE:] = pick(odd, left, right)
    odd_ref[TILE:] = pick(odd, right, left)


def pack_kernel(member_ref, static_ref, first_ref, even_ref, odd_ref, own_ref):
    first_ref[...] = member_ref[0]
    second = member_ref[1].reshape(2304, 128)
    even_ref[:2304] = second
    odd_ref[:2304] = second
    packed = halves(static_ref[...])
    own_ref[...] = packed
    pack_slabs(packed, even_ref, odd_ref)


def first_y_kernel(row_m, row_s, taps_ref, sent_ref, own_ref, odd_ref, even_ref, to_even_ref, to_odd_ref, out_ref):
    member = band_swapped(taps_ref[row_m : row_m + 1], "ty")
    static = band(taps_ref[row_s : row_s + 1], TILE, 112)

    def member_line(x):
        at = pl.ds(pl.multiple_of(x * TILE, TILE), TILE)
        return jnp.concatenate([even_ref[at], sent_ref[at], odd_ref[at]], axis=0)

    def member_store(x, out):
        out = out.astype(BF)
        to_even_ref[x] = out
        to_odd_ref[x] = out

    along_y(member, member_line, TILE, member_store)

    def static_line(x):
        at = pl.ds(pl.multiple_of(2304 + x * SLAB, SLAB), SLAB)
        left, right = sides(even_ref[at], odd_ref[at], "ty")
        return jnp.concatenate([left, own_ref[x], right], axis=0)

    def static_store(x, out):
        out_ref[x] = out.astype(BF)

    along_y(static, static_line, 24, static_store)
    pack_x(out_ref[...], to_even_ref, to_odd_ref)


def first_x_kernel(row, taps_ref, own_ref, even_ref, odd_ref, out_ref):
    matrix = band_swapped(taps_ref[row : row + 1], "tx")
    for c in range(0, TILE, 16):
        at = slice(c, c + 16)
        out_ref[:, at] = along_x(matrix, [even_ref[:, at], own_ref[:, at], odd_ref[:, at]])


def second_y(row, taps_ref, own_ref, even_ref, odd_ref, store):
    matrix = band_swapped(taps_ref[row : row + 1], "ty")

    def line(x):
        return jnp.concatenate([even_ref[x], own_ref[x], odd_ref[x]], axis=0)

    along_y(matrix, line, TILE, store)


def second_x(cols, rows, taps_ref, own_ref, even_ref, odd_ref, s_ref, block):
    matrix = band_swapped(taps_ref[rows[0] : rows[0] + 1], "tx")
    matrix_s = band(taps_ref[rows[1] : rows[1] + 1], 24, 72)
    for c in range(cols[0], cols[1], 16):
        at = slice(c, c + 16)
        b = along_x(matrix, [even_ref[:TILE, at], own_ref[:TILE, at], odd_ref[:TILE, at]])
        left, right = sides(even_ref[TILE:, at], odd_ref[TILE:, at], "tx")
        lines = static_parts(left, s_ref[:, at], right)
        block(at, b, along_x(matrix_s, [lines]))


def static_block(static_ref):
    full = static_ref[...]
    cols = jnp.where(lax.axis_index("mem") == 0, full[:, :64], full[:, 64:])
    zero = jnp.zeros_like(cols)
    return jnp.concatenate([jnp.concatenate([cols, zero], axis=1), jnp.concatenate([zero, cols], axis=1)], axis=0)


def dot_t(a, b):
    return lax.dot_general(a, b, (((1,), (1,)), ((), ())), preferred_element_type=F32)


def forward_a_kernel(row, taps_ref, own_ref, even_ref, odd_ref, pert_ref, vert_ref, out_ref, filtered):
    def store(x, out):
        filtered[x] = out.astype(BF)

    second_y(row, taps_ref, own_ref, even_ref, odd_ref, store)
    vert = vert_ref[...]

    def step(i, carry):
        at = pl.ds(8 * i, 8)
        local = dot_t(filtered[at].reshape(384, 128), vert).reshape(8, TILE, 128)
        out_ref[at] = pert_ref[0, at].astype(F32) * local
        return carry

    lax.fori_loop(0, 6, step, 0, unroll=6)


def forward_b_kernel(
    cols, rows, taps_ref, own_ref, even_ref, odd_ref, s_ref, first_ref, pert_ref, vert_ref, static_ref,
    after_ref, kept_ref, sent_ref
):
    vert = vert_ref[...]
    static_mat = static_block(static_ref)

    def block(at, b, s):
        total = first_ref[:, at]
        total += pert_ref[1, :, at].astype(F32) * dot_t(b.reshape(768, 128), vert).reshape(TILE, 16, 128)
        static = dot_t(s.reshape(384, 128), static_mat)
        total += jnp.concatenate([static[:, :128], static[:, 128:]], axis=0).reshape(TILE, 16, 128)
        to = slice(at.start - cols[0], at.stop - cols[0])
        kept_ref[:, to] = total
        sent_ref[:, to] = total.astype(BF)

    second_x(cols, rows, taps_ref, own_ref, even_ref, odd_ref, s_ref, block)


def residual_kernel(
    kept0, came0, kept1, came1, kept2, came2, dep_ref, weight_ref, pert_ref, vert_ref, static_ref, even_ref, odd_ref, own_ref, b_ref
):
    vert = vert_ref[...]
    static_mat = static_block(static_ref)

    def step(i, carry):
        res = []
        for x in (4 * i, 24 + 4 * i):
            at = pl.ds(x, 4)
            pairs = ((kept0, came0), (kept1, came1), (kept2, came2))
            parts = [kept[at] + came[at].astype(F32) for kept, came in pairs]
            total = jnp.concatenate(parts, axis=1)
            r = (weight_ref[at].astype(F32) * (total - dep_ref[at].astype(F32))).astype(BF)
            r32 = r.astype(F32)
            res.append(r.reshape(192, 128))
            first = (pert_ref[0, at].astype(F32) * r32).astype(BF).reshape(192, 128)
            second = (pert_ref[1, at].astype(F32) * r32).astype(BF).reshape(192, 128)
            back = dot(first, vert).astype(BF).reshape(4, TILE, 128)
            even_ref[at] = back
            odd_ref[at] = back
            b_ref[at] = dot(second, vert).astype(BF).reshape(4, TILE, 128)
        static = dot(jnp.concatenate(res, axis=1), static_mat).astype(BF)
        own_ref[pl.ds(4 * i, 4)] = static.reshape(4, TILE, 128)
        return carry

    lax.fori_loop(0, 6, step, 0, unroll=6)
    pack_x(own_ref[...], even_ref, odd_ref)


def back_x_kernel(
    rows, taps_ref, sent_ref, own_ref, even_ref, odd_ref, after_ref, to_even_ref, to_odd_ref, slab_ref, out_ref
):
    member = band_swapped(taps_ref[rows[0] : rows[0] + 1], "tx")
    static = band(taps_ref[rows[1] : rows[1] + 1], 24, 72)
    for c in range(0, TILE, 16):
        at = slice(c, c + 16)
        out = along_x(member, [even_ref[:TILE, at], sent_ref[:TILE, at], odd_ref[:TILE, at]])
        to_even_ref[:TILE, at] = out
        to_odd_ref[:, at] = out
        left, right = sides(even_ref[TILE:, at], odd_ref[TILE:, at], "tx")
        out_ref[:, at] = along_x(static, [static_parts(left, own_ref[:, at], right)])
    packed = out_ref[...]
    right = packed[:, 16:48].reshape(16, TILE, 128)
    left = packed[:, :SLAB].reshape(16, TILE, 128)
    odd, _ = place("ty")
    to_even_ref[TILE:] = pick(odd, left, right)
    slab_ref[...] = pick(odd, right, left)


def back_y_kernel(row, taps_ref, own_ref, even_ref, odd_ref, out_ref):
    def store(x, out):
        out_ref[x] = out.astype(BF)

    second_y(row, taps_ref, own_ref, even_ref, odd_ref, store)


def last_b_kernel(row, taps_ref, own_ref, even_ref, odd_ref, member_ref, member_out, member, sems):
    matrix = band_swapped(taps_ref[row : row + 1], "tx")
    copies = []
    for i in range(3):
        at = slice(16 * i, 16 * i + 16)
        b = along_x(matrix, [even_ref[:, at], own_ref[:, at], odd_ref[:, at]])
        member[i] = (member_ref[1, :, at].astype(F32) + b.astype(F32)).astype(BF)
        copies.append(pltpu.make_async_copy(member.at[i], member_out.at[1, :, at], sems.at[i]))
        copies[i].start()
    for copy in copies:
        copy.wait()


def last_a_kernel(
    rows, taps_ref, own_ref, even_ref, odd_ref, slab_ref, s_ref, member_ref, control_ref, begun_ref,
    static_out, member_out, static, member, sems
):
    copies = []

    def send(source, target):
        copies.append(pltpu.make_async_copy(source, target, sems.at[len(copies)]))
        copies[-1].start()

    matrix = band(taps_ref[rows[1] : rows[1] + 1], TILE, 112)
    slabs = [r.reshape(24, SLAB, 128) for r in (even_ref[TILE:], slab_ref[...])]
    left, right = sides(slabs[0], slabs[1], "ty")
    for x in range(0, 24, 2):
        lines = [jnp.concatenate([left[k], s_ref[k], right[k]], axis=0) for k in (x, x + 1)]
        out = dot(matrix, jnp.concatenate(lines, axis=1)).astype(BF).astype(F32)
        for k in (0, 1):
            both = (control_ref[x + k].astype(F32) + out[:, 128 * k : 128 * k + 128]).astype(BF)
            static[x + k] = both[:, :64]
            static[x + k + 24] = both[:, 64:]
        if x % 12 == 10:
            for part in (pl.ds(x - 10, 12), pl.ds(x + 14, 12)):
                send(static.at[part], static_out.at[part])
    matrix = band_swapped(taps_ref[rows[0] : rows[0] + 1], "ty")
    for first in range(0, TILE, 12):

        def line(x):
            x = first + x
            return jnp.concatenate([even_ref[x], own_ref[x], odd_ref[x]], axis=0)

        def store(x, out):
            x = first + x
            member[x] = (member_ref[0, x].astype(F32) + out.astype(BF).astype(F32)).astype(BF)

        along_y(matrix, line, 12, store)
        part = pl.ds(first, 12)
        send(member.at[part], member_out.at[0, part])
    for copy in copies:
        copy.wait()


def swaps_y(even, *odd):
    n = lax.axis_size("ty")
    first = [(i, i ^ 1) for i in range(n)]
    second = [(i, (i + 1) % n if i % 2 else (i - 1) % n) for i in range(n)]
    return (lax.ppermute(even, "ty", first),) + tuple(lax.ppermute(part, "ty", second) for part in odd)


def swaps_x(even, odd):
    n, m = lax.axis_size("tx"), lax.axis_size("ty")
    first = [(i, i ^ 1) for i in range(n)]
    second = []
    for i in range(n):
        other = i + 1 if i % 2 else i - 1
        for j in range(m):
            second.append((i * m + j, i * m + (j ^ 1) if i in (0, n - 1) else other * m + j))
    return lax.ppermute(even, "tx", first), lax.ppermute(odd, ("tx", "ty"), second)


def first_filters(taps, a, to_even, to_odd, own):
    a_halo = swaps_x(a, a)
    b_halo = swaps_y(to_even, to_odd)[::-1]
    tile = (TILE, TILE, 128)
    b_to_even, b_to_odd, s = call(
        functools.partial(first_y_kernel, 1, 3),
        (shape(60, TILE, 128), shape(60, TILE, 128), shape(24, TILE, 128)),
        (taps, to_even, own) + b_halo,
        700_000_000,
    )
    b_halo = swaps_x(b_to_even, b_to_odd)
    (a,) = call(functools.partial(first_x_kernel, 0), (shape(*tile),), (taps, a) + a_halo, 500_000_000)
    a_halo = swaps_y(a, a)
    return (a,) + a_halo, (b_to_even,) + b_halo + (s,)


def body(
    static_control,
    member_control,
    perturbations,
    departures,
    obs_weight,
    static_kx,
    static_ky,
    local_kx,
    local_ky,
    static_vertical,
    local_vertical,
):
    (taps,) = call(
        taps_kernel, (shape(8, 256, dtype=F32),), (local_kx, local_ky, static_kx, static_ky), BRIEF
    )
    tile = (TILE, TILE, 128)
    sent_shapes = (shape(3072, 128), shape(3072, 128), shape(24, TILE, 128))

    a, to_even, to_odd, control = call(
        pack_kernel, (shape(*tile),) + sent_shapes, (member_control, static_control), 1_000_000
    )
    a, b = first_filters(taps, a, to_even, to_odd, control)
    (first,) = call(
        functools.partial(forward_a_kernel, 1), (shape(*tile, dtype=F32),),
        (taps,) + a + (perturbations, local_vertical), 800_000_000, [pltpu.VMEM(tile, BF)],
    )
    size = lax.axis_size("mem")
    parts, sent = (), first
    for cols, cost in (((0, 16), 700_000_000), ((16, 32), LONG), ((32, TILE), LONG)):
        wide = (TILE, cols[1] - cols[0], 128)
        args = (taps,) + b + (first, perturbations, local_vertical, static_vertical, sent)
        kept, sent = call(
            functools.partial(forward_b_kernel, cols, (0, 2)), (shape(*wide, dtype=F32), shape(*wide)),
            args, cost, in_any=(len(args) - 1,),
        )
        parts += (kept, lax.ppermute(sent, "mem", [(i, size - 1 - i) for i in range(size)]))

    to_even, to_odd, own, b = call(
        residual_kernel, (shape(60, TILE, 128), shape(60, TILE, 128), shape(24, TILE, 128), shape(*tile)),
        parts + (departures, obs_weight, perturbations, local_vertical, static_vertical), 400_000_000,
    )
    a = (to_even, own) + swaps_x(to_even, to_odd)
    (b,) = call(functools.partial(back_y_kernel, 5), (shape(*tile),), (taps, b) + swaps_y(b, b), BRIEF)
    b_halo = swaps_x(b, b)
    args = (taps,) + a + (b,)
    to_even, to_odd, slab, s = call(
        functools.partial(back_x_kernel, (4, 6)),
        (shape(64, TILE, 128), shape(*tile), shape(16, TILE, 128), shape(24, TILE, 128)), args, LONG,
        in_any=(len(args) - 1,),
    )
    a = (to_even,) + swaps_y(to_even, to_odd, slab) + (s,)
    (begun,) = call(
        functools.partial(last_b_kernel, 4), (shape(2, *tile),), (taps, b) + b_halo + (member_control,), LONG,
        [pltpu.VMEM((3, TILE, 16, 128), BF), pltpu.SemaphoreType.DMA((3,))], out_any=(0,),
    )
    args = (taps,) + a + (member_control, control, begun)
    return tuple(call(
        functools.partial(last_a_kernel, (5, 7)), (shape(TILE, TILE, 64), shape(2, *tile)), args, 700_000_000,
        [pltpu.VMEM((TILE, TILE, 64), BF), pltpu.VMEM(tile, BF), pltpu.SemaphoreType.DMA((8,))],
        in_any=(len(args) - 1,), out_any=(0, 1), aliases={len(args) - 1: 1},
    ))


def solution(mesh):
    return jax.shard_map(
        body,
        mesh=mesh,
        in_specs=(
            P("tx", "ty", "mem"),
            P("mem", "tx", "ty", None),
            P("mem", "tx", "ty", None),
            P("tx", "ty", None),
            P("tx", "ty", None),
            P(),
            P(),
            P(),
            P(),
            P(),
            P(),
        ),
        out_specs=(P("tx", "ty", "mem"), P("mem", "tx", "ty", None)),
        check_vma=False,
    )
```
